32 devices in a mesh: segment: 16 (over z, x, core), band: 2 (over y).
Axes of the slice: x: 2, y: 2, z: 4, core: 2. Of those that a mesh axis runs over, the one named last changes fastest.
Arguments:
- first_input: bfloat16 [16, 16, 128, 256], P('segment', 'band'), may hold values from -6 to 6
- stashed: bfloat16 [16, 2, 16, 128, 256], P('segment', None, 'band'), may hold values from -6 to 6
- first_grad: bfloat16 [16, 16, 128, 256], P('segment', 'band'), may hold values from -6 to 6
- weight_now: bfloat16 [16, 3, 3, 256, 256], P('segment'), may hold values from -5 to 5
- weight_old: bfloat16 [16, 3, 3, 256, 256], P('segment'), may hold values from -5 to 5
- momentum: float32 [16, 3, 3, 256, 256], P('segment'), may hold values from -6 to 6
- slot_plan: int32 [2, 16], P(None, 'segment'), may hold values from 0 to 1
- next_input: bfloat16 [16, 128, 256], P('band'), may hold values from -6 to 6
- next_grad: bfloat16 [16, 128, 256], P('band'), may hold values from -6 to 6
Outputs:
- act_out: bfloat16 [16, 16, 128, 256], P('segment', 'band')
- grad_out: bfloat16 [16, 16, 128, 256], P('segment', 'band')
- weight_now_out: bfloat16 [16, 3, 3, 256, 256], P('segment')
- weight_old_out: bfloat16 [16, 3, 3, 256, 256], P('segment')
- momentum_out: float32 [16, 3, 3, 256, 256], P('segment')
The draws below stay inside these ranges and needn't reach their ends.
All inputs are finite; a program needn't handle non-finite values.
Results may differ from the reference program's by a relative error of at most 0.009.
Values may be sent and summed in bfloat16 or wider, within the bound.
No kernel may reach another device: no remote copies, remote signals or barrier semaphores. Data moves between devices by JAX's collectives and lax.ppermute only.
A program may use at most 128 MiB of HBM per device.

```python
import math
import jax
import jax.numpy as jnp
from jax import lax

C = 256
WCOL = 128
SLOTS = 2
SEGMENTS = 16
H = 16


def place_ends(drawn, rng, least, largest):
    longest = drawn.shape.index(max(drawn.shape))
    spots = []
    for shift in (0, 1):
        where = [jax.random.randint(jax.random.fold_in(rng, axis), (), 0, length) for axis, length in enumerate(drawn.shape)]
        where[longest] = (where[longest] + shift) % drawn.shape[longest]
        spots.append(tuple(where))
    return drawn.at[spots[0]].set(least).at[spots[1]].set(largest)


def level_of(own_key, dims, split, low, largest):
    level, own = 1.0, jax.random.fold_in(own_key, 6)
    for axis_at, parts in split:
        heights = jnp.exp(jax.random.uniform(jax.random.fold_in(own, axis_at), (parts,), jnp.float32, low / len(split), largest / len(split)))
        level = level * jnp.repeat(heights, dims[axis_at] // parts).reshape([-1 if axis == axis_at else 1 for axis in range(len(dims))])
    return level


def gaussian(stream_key, dims, scale, bound, split=(), kind=jnp.bfloat16):
    drawn = jax.random.normal(stream_key, dims, jnp.float32) * scale
    if len(split) > 0:
        drawn = level_of(stream_key, dims, split, -0.22, 0.18) * drawn
    return jnp.clip(drawn, min=-bound, max=bound).astype(kind)


def setup_inputs(seed: int = 0) -> dict:
    streams_of = jax.random.split(jax.random.key(seed), 10)
    return {
        "first_input": gaussian(streams_of[0], (SEGMENTS, H, WCOL, C), 1.0, 6.0, ((0, 16), (1, 2))),
        "stashed": gaussian(streams_of[1], (SEGMENTS, SLOTS, H, WCOL, C), 1.0, 6.0, ((0, 16), (2, 2))),
        "first_grad": gaussian(streams_of[2], (SEGMENTS, H, WCOL, C), 1.0, 6.0, ((0, 16), (1, 2))),
        "weight_now": gaussian(streams_of[3], (SEGMENTS, 3, 3, C, C), 1.0, 5.0, ((0, 16),)),
        "weight_old": gaussian(streams_of[4], (SEGMENTS, 3, 3, C, C), 1.0, 5.0, ((0, 16),)),
        "momentum": gaussian(streams_of[5], (SEGMENTS, 3, 3, C, C), 1.0, 6.0, ((0, 16),), jnp.float32),
        "slot_plan": place_ends(jax.random.randint(streams_of[6], (2, SEGMENTS), 0, SLOTS), jax.random.fold_in(streams_of[6], 1), 0, SLOTS - 1).astype(jnp.int32),
        "next_input": gaussian(streams_of[7], (H, WCOL, C), 1.0, 6.0, ((0, 2),)),
        "next_grad": gaussian(streams_of[8], (H, WCOL, C), 1.0, 6.0, ((0, 2),)),
    }


def row_patches(extended, rows):
    wcol = extended.shape[1]
    padded = jnp.pad(extended, ((0, 0), (1, 1), (0, 0)))
    taps = [padded[ky:ky + rows, kx:kx + wcol, :] for ky in range(3) for kx in range(3)]
    return jnp.concatenate(taps, axis=2).reshape(rows * wcol, -1)

def silu_slope(value):
    sig = jax.nn.sigmoid(value)
    return sig * (1.0 + value * (1.0 - sig))

def segment_tick(inputs):
    x_in, stash, grad, w_now, w_old, moment, slot = inputs
    factor = 1.0 / math.sqrt(9 * C)
    rows = x_in.shape[0]
    wcol = x_in.shape[1]
    flat_now = w_now.reshape(9 * C, C)
    flat_old = w_old.reshape(9 * C, C)
    flip_old = w_old[::-1, ::-1].transpose(0, 1, 3, 2).reshape(9 * C, C)
    ext = jnp.pad(x_in, ((1, 1), (0, 0), (0, 0)))
    pre = jnp.dot(row_patches(ext, rows), flat_now, preferred_element_type=jnp.float32) * factor
    out = jax.nn.silu(pre).astype(jnp.bfloat16).reshape(rows, wcol, C)
    chosen = lax.dynamic_index_in_dim(stash, slot, 0, keepdims=False)
    patches = row_patches(jnp.pad(chosen, ((1, 1), (0, 0), (0, 0))), rows)
    back = jnp.dot(patches, flat_old, preferred_element_type=jnp.float32) * factor
    slope_grad = (grad.reshape(-1, C).astype(jnp.float32) * silu_slope(back)).astype(jnp.bfloat16)
    slope_ext = jnp.pad(slope_grad.reshape(rows, wcol, C), ((1, 1), (0, 0), (0, 0)))
    in_grad = jnp.dot(row_patches(slope_ext, rows), flip_old, preferred_element_type=jnp.float32) * factor
    in_grad = in_grad.astype(jnp.bfloat16).reshape(rows, wcol, C)
    kgrad = lax.dot_general(patches, slope_grad, (((0,), (0,)), ((), ())), preferred_element_type=jnp.float32) * factor
    new_moment = 0.9 * moment + kgrad.reshape(moment.shape)
    new_weight = (w_now.astype(jnp.float32) - 0.05 * new_moment).astype(jnp.bfloat16)
    new_stash = lax.dynamic_update_index_in_dim(stash, x_in, slot, 0)
    return (out, in_grad, new_weight, new_moment, new_stash)

def reference(first_input, stashed, first_grad, weight_now, weight_old, momentum, slot_plan, next_input, next_grad):
    out_one, grad_one, weight_one, moment_one, stash_one = lax.map(segment_tick, (first_input, stashed, first_grad, weight_now, weight_old, momentum, slot_plan[0].astype(jnp.int32)))
    input_two = jnp.concatenate([next_input[None], out_one[:-1]], axis=0)
    grad_two = jnp.concatenate([grad_one[1:], next_grad[None]], axis=0)
    out_two, grad_back, weight_two, moment_two, stash_two = lax.map(segment_tick, (input_two, stash_one, grad_two, weight_one, weight_now, moment_one, slot_plan[1].astype(jnp.int32)))
    return (out_two, grad_back, weight_two, weight_one, moment_two)
```

```python
import math

import jax
import jax.numpy as jnp
from jax import lax
from jax.sharding import PartitionSpec as P

C = 256


def padded_2(block, sides, width):
    for axis, dim in sides:
        count = lax.axis_size(axis)
        forward = [(i, i + 1) for i in range(count - 1)]
        backward = [(target, source) for source, target in forward]
        low = lax.ppermute(
            lax.slice_in_dim(block, block.shape[dim] - width, None, axis=dim), axis, forward
        )
        high = lax.ppermute(lax.slice_in_dim(block, 0, width, axis=dim), axis, backward)
        block = jnp.concatenate([low, block, high], axis=dim)
    return block


def passed_along(array, axis, by):
    length = lax.axis_size(axis)
    pairs = [(i, i + by) for i in range(length) if 0 <= i + by < length]
    return lax.ppermute(array, axis, pairs)


def row_patches(extended, rows):
    wcol = extended.shape[1]
    padded = jnp.pad(extended, ((0, 0), (1, 1), (0, 0)))
    taps = [padded[ky : ky + rows, kx : kx + wcol, :] for ky in range(3) for kx in range(3)]
    return jnp.concatenate(taps, axis=2).reshape(rows * wcol, -1)


def silu_slope(value):
    sig = jax.nn.sigmoid(value)
    return sig * (1.0 + value * (1.0 - sig))


def forward_part(x_in, flat_now, factor):
    rows, wcol = (x_in.shape[0], x_in.shape[1])
    ext = padded_2(x_in, (("band", 0),), 1)
    pre = jnp.dot(row_patches(ext, rows), flat_now, preferred_element_type=jnp.float32) * factor
    return jax.nn.silu(pre).astype(jnp.bfloat16).reshape(rows, wcol, C)


def backward_part(chosen, grad, w_old, factor):
    rows, wcol = (chosen.shape[0], chosen.shape[1])
    flat_old = w_old.reshape(9 * C, C)
    flip_old = w_old[::-1, ::-1].transpose(0, 1, 3, 2).reshape(9 * C, C)
    ext = padded_2(chosen, (("band", 0),), 1)
    patches = row_patches(ext, rows)
    back = jnp.dot(patches, flat_old, preferred_element_type=jnp.float32) * factor
    slope_grad = (grad.reshape(-1, C) * silu_slope(back)).astype(jnp.bfloat16)
    slope_ext = padded_2(slope_grad.reshape(rows, wcol, C), (("band", 0),), 1)
    kgrad = (
        lax.dot_general(
            patches, slope_grad, (((0,), (0,)), ((), ())), preferred_element_type=jnp.float32
        )
        * factor
    )
    in_grad = (
        jnp.dot(row_patches(slope_ext, rows), flip_old, preferred_element_type=jnp.float32) * factor
    )
    return (in_grad.astype(jnp.bfloat16).reshape(rows, wcol, C), kgrad)


def update_part(kgrad, w_now, moment):
    flat_now = w_now.reshape(9 * C, C).astype(jnp.float32)
    total = lax.psum(kgrad.astype(jnp.bfloat16), "band").astype(jnp.float32)
    new_moment = 0.9 * moment + total
    new_flat = (flat_now - 0.05 * new_moment).astype(jnp.bfloat16)
    return (new_flat.reshape(3, 3, C, C), new_moment)


def body(
    first_input,
    stashed,
    first_grad,
    weight_now,
    weight_old,
    momentum,
    slot_plan,
    next_input,
    next_grad,
):
    factor = 1.0 / math.sqrt(9 * C)
    segment_pos = lax.axis_index("segment")
    last_pos = lax.axis_size("segment") - 1
    x_in = first_input[0]
    stash = stashed[0]
    grad = first_grad[0]
    w_now = weight_now[0]
    w_old = weight_old[0]
    moment = momentum[0].reshape(9 * C, C)
    slots = slot_plan[:, 0]
    for tick in range(2):
        if tick == 1:
            arrived = passed_along(out_acts, "segment", 1)
            x_in = jnp.where(segment_pos == 0, next_input, arrived)
            returned = passed_along(in_grad, "segment", -1)
            grad = jnp.where(segment_pos == last_pos, next_grad, returned)
        out_acts = forward_part(x_in, w_now.reshape(9 * C, C), factor)
        chosen = lax.dynamic_index_in_dim(stash, slots[tick], 0, keepdims=False)
        in_grad, kgrad = backward_part(chosen, grad, w_old, factor)
        stash = lax.dynamic_update_index_in_dim(stash, x_in, slots[tick], 0)
        new_weight, moment = update_part(kgrad, w_now, moment)
        w_old = w_now
        w_now = new_weight
    return (out_acts[None], in_grad[None], w_now[None], w_old[None], moment.reshape(1, 3, 3, C, C))


SWAP = [(0, 1), (1, 0)]
DIMS = ("NHWC", "HWIO", "NHWC")


def conv_rows(extended, kernel):
    return lax.conv_general_dilated(
        extended[None], kernel, (1, 1), ((0, 0), (1, 1)),
        dimension_numbers=DIMS, preferred_element_type=jnp.float32,
    )[0]


def joined(own, other, top):
    return jnp.where(top, jnp.concatenate([own, other], 0), jnp.concatenate([other, own], 0))


def outer_zero(rows, top):
    zero = jnp.zeros((1,) + rows.shape[1:], rows.dtype)
    return joined(zero, rows, top)


def whole_backward(x_full, grad_full, w_back, factor):
    ext = jnp.pad(x_full, ((1, 1), (0, 0), (0, 0)))
    back = conv_rows(ext, w_back) * factor
    dz = (grad_full * silu_slope(back)).astype(jnp.bfloat16)
    kgrad = lax.conv_general_dilated(
        x_full[None], dz[None], (1, 1), ((1, 1), (1, 1)),
        dimension_numbers=("CHWN", "IHWO", "HWNC"), preferred_element_type=jnp.float32,
    )
    return dz, kgrad * factor


def two_band_body(
    first_input, stashed, first_grad, weight_now, weight_old, momentum, slot_plan,
    next_input, next_grad,
):
    factor = 1.0 / math.sqrt(9 * C)
    segment_pos = lax.axis_index("segment")
    last_pos = lax.axis_size("segment") - 1
    top = lax.axis_index("band") == 0
    x_in, stash, grad = first_input[0], stashed[0], first_grad[0]
    w_now, w_old, moment = weight_now[0], weight_old[0], momentum[0]
    rows = x_in.shape[0]
    slots = slot_plan[:, 0]

    def swapped(array):
        return lax.ppermute(array, "band", SWAP)

    xs1 = lax.dynamic_index_in_dim(stash, slots[0], 0, keepdims=False)
    xs2 = jnp.where(
        slots[0] == slots[1], x_in, lax.dynamic_index_in_dim(stash, slots[1], 0, keepdims=False)
    )
    xs1_other = swapped(xs1)
    grad_other = swapped(grad)
    edge2 = jnp.where(top, x_in[rows - 2 :], x_in[:2])
    edge1 = jnp.where(top, next_input[rows - 1 :], next_input[:1])
    halo = swapped(jnp.concatenate([edge2, edge1], 0))
    xs2_other = swapped(xs2)
    last = 2 * last_pos
    next_grad_other = lax.ppermute(
        next_grad, ("segment", "band"), [(last, last + 1), (last + 1, last)]
    )

    ext = outer_zero(joined(x_in, halo[:2], top), top)
    y1 = jax.nn.silu(conv_rows(ext, w_now) * factor).astype(jnp.bfloat16)
    arrived = passed_along(y1, "segment", 1)
    x2 = jnp.where(segment_pos == 0, joined(next_input, halo[2:], top), arrived)

    flip_old = w_old[::-1, ::-1].transpose(0, 1, 3, 2)
    flip_now = w_now[::-1, ::-1].transpose(0, 1, 3, 2)
    dz1, kgrad1 = whole_backward(
        joined(xs1, xs1_other, top), joined(grad, grad_other, top), w_old, factor
    )
    dx1 = conv_rows(jnp.pad(dz1, ((1, 1), (0, 0), (0, 0))), flip_old) * factor
    returned = passed_along(dx1.astype(jnp.bfloat16), "segment", -1)
    g2 = jnp.where(segment_pos == last_pos, joined(next_grad, next_grad_other, top), returned)
    m1 = 0.9 * moment + kgrad1
    w1 = (w_now.astype(jnp.float32) - 0.05 * m1).astype(jnp.bfloat16)

    act = jax.nn.silu(conv_rows(outer_zero(x2, top), w1) * factor).astype(jnp.bfloat16)
    dz2, kgrad2 = whole_backward(joined(xs2, xs2_other, top), g2, w_now, factor)
    dz2 = jnp.pad(dz2, ((1, 1), (0, 0), (0, 0)))
    dz2_own = jnp.where(top, dz2[: rows + 2], dz2[rows:])
    dx2 = (conv_rows(dz2_own, flip_now) * factor).astype(jnp.bfloat16)
    m2 = 0.9 * m1 + kgrad2
    w2 = (w1.astype(jnp.float32) - 0.05 * m2).astype(jnp.bfloat16)
    return act[None], dx2[None], w2[None], w1[None], m2[None]


def solution(mesh):
    placed = (
        P("segment", "band", None, None),
        P("segment", None, "band", None, None),
        P("segment", "band", None, None),
        P("segment", None, None, None, None),
        P("segment", None, None, None, None),
        P("segment", None, None, None, None),
        P(None, "segment"),
        P("band", None, None),
        P("band", None, None),
    )
    return jax.shard_map(
        two_band_body if mesh.shape["band"] == 2 else body,
        mesh=mesh,
        in_specs=placed,
        out_specs=(
            P("segment", "band", None, None),
            P("segment", "band", None, None),
            P("segment", None, None, None, None),
            P("segment", None, None, None, None),
            P("segment", None, None, None, None),
        ),
        check_vma=False,
    )
```

```python
import math

import jax
import jax.numpy as jnp
from jax import lax
from jax.experimental import pallas as pl
from jax.experimental.pallas import tpu as pltpu
from jax.sharding import PartitionSpec as P

C = 256


def padded_2(block, sides, width):
    for axis, dim in sides:
        count = lax.axis_size(axis)
        forward = [(i, i + 1) for i in range(count - 1)]
        backward = [(target, source) for source, target in forward]
        low = lax.ppermute(
            lax.slice_in_dim(block, block.shape[dim] - width, None, axis=dim), axis, forward
        )
        high = lax.ppermute(lax.slice_in_dim(block, 0, width, axis=dim), axis, backward)
        block = jnp.concatenate([low, block, high], axis=dim)
    return block


def passed_along(array, axis, by):
    length = lax.axis_size(axis)
    pairs = [(i, i + by) for i in range(length) if 0 <= i + by < length]
    return lax.ppermute(array, axis, pairs)


def row_patches(extended, rows):
    wcol = extended.shape[1]
    padded = jnp.pad(extended, ((0, 0), (1, 1), (0, 0)))
    taps = [padded[ky : ky + rows, kx : kx + wcol, :] for ky in range(3) for kx in range(3)]
    return jnp.concatenate(taps, axis=2).reshape(rows * wcol, -1)


def silu_slope(value):
    sig = jax.nn.sigmoid(value)
    return sig * (1.0 + value * (1.0 - sig))


def forward_part(x_in, flat_now, factor):
    rows, wcol = (x_in.shape[0], x_in.shape[1])
    ext = padded_2(x_in, (("band", 0),), 1)
    pre = jnp.dot(row_patches(ext, rows), flat_now, preferred_element_type=jnp.float32) * factor
    return jax.nn.silu(pre).astype(jnp.bfloat16).reshape(rows, wcol, C)


def backward_part(chosen, grad, w_old, factor):
    rows, wcol = (chosen.shape[0], chosen.shape[1])
    flat_old = w_old.reshape(9 * C, C)
    flip_old = w_old[::-1, ::-1].transpose(0, 1, 3, 2).reshape(9 * C, C)
    ext = padded_2(chosen, (("band", 0),), 1)
    patches = row_patches(ext, rows)
    back = jnp.dot(patches, flat_old, preferred_element_type=jnp.float32) * factor
    slope_grad = (grad.reshape(-1, C) * silu_slope(back)).astype(jnp.bfloat16)
    slope_ext = padded_2(slope_grad.reshape(rows, wcol, C), (("band", 0),), 1)
    kgrad = (
        lax.dot_general(
            patches, slope_grad, (((0,), (0,)), ((), ())), preferred_element_type=jnp.float32
        )
        * factor
    )
    in_grad = (
        jnp.dot(row_patches(slope_ext, rows), flip_old, preferred_element_type=jnp.float32) * factor
    )
    return (in_grad.astype(jnp.bfloat16).reshape(rows, wcol, C), kgrad)


def update_part(kgrad, w_now, moment):
    flat_now = w_now.reshape(9 * C, C).astype(jnp.float32)
    total = lax.psum(kgrad.astype(jnp.bfloat16), "band").astype(jnp.float32)
    new_moment = 0.9 * moment + total
    new_flat = (flat_now - 0.05 * new_moment).astype(jnp.bfloat16)
    return (new_flat.reshape(3, 3, C, C), new_moment)


def body(
    first_input,
    stashed,
    first_grad,
    weight_now,
    weight_old,
    momentum,
    slot_plan,
    next_input,
    next_grad,
):
    factor = 1.0 / math.sqrt(9 * C)
    segment_pos = lax.axis_index("segment")
    last_pos = lax.axis_size("segment") - 1
    x_in = first_input[0]
    stash = stashed[0]
    grad = first_grad[0]
    w_now = weight_now[0]
    w_old = weight_old[0]
    moment = momentum[0].reshape(9 * C, C)
    slots = slot_plan[:, 0]
    for tick in range(2):
        if tick == 1:
            arrived = passed_along(out_acts, "segment", 1)
            x_in = jnp.where(segment_pos == 0, next_input, arrived)
            returned = passed_along(in_grad, "segment", -1)
            grad = jnp.where(segment_pos == last_pos, next_grad, returned)
        out_acts = forward_part(x_in, w_now.reshape(9 * C, C), factor)
        chosen = lax.dynamic_index_in_dim(stash, slots[tick], 0, keepdims=False)
        in_grad, kgrad = backward_part(chosen, grad, w_old, factor)
        stash = lax.dynamic_update_index_in_dim(stash, x_in, slots[tick], 0)
        new_weight, moment = update_part(kgrad, w_now, moment)
        w_old = w_now
        w_now = new_weight
    return (out_acts[None], in_grad[None], w_now[None], w_old[None], moment.reshape(1, 3, 3, C, C))


SWAP = [(0, 1), (1, 0)]
BF16 = jnp.bfloat16
F32 = jnp.float32
NT = (((1,), (1,)), ((), ()))
TN = (((0,), (0,)), ((), ()))
MIB = 2**20


def vmem(count):
    return [pl.BlockSpec(memory_space=pltpu.VMEM)] * count


def anywhere(count):
    return [pl.BlockSpec(memory_space=pl.ANY)] * count


SMEM = pl.BlockSpec(memory_space=pltpu.SMEM)


def call(kernel, outs, in_specs, out_specs, scratch, macs, limit=24):
    return pl.pallas_call(
        kernel,
        out_shape=[jax.ShapeDtypeStruct(shape, kind) for shape, kind in outs],
        in_specs=in_specs,
        out_specs=out_specs,
        scratch_shapes=scratch,
        compiler_params=pltpu.CompilerParams(vmem_limit_bytes=limit * MIB),
        cost_estimate=pl.CostEstimate(
            flops=2 * macs, bytes_accessed=MIB, transcendentals=0
        ),
    )


def conv_rows(rows_of, start, count, taps):
    lhs = [rows_of[pl.ds(start + ky, count)] for ky in range(3)]
    wcol = lhs[0].shape[1]
    lhs = jnp.concatenate([part.reshape(count * wcol, C) for part in lhs], axis=1)
    left, mid, right = (
        part.reshape(count, wcol, C) for part in (taps(lhs, 0), taps(lhs, 1), taps(lhs, 2))
    )
    col = lax.broadcasted_iota(jnp.int32, mid.shape, 1)
    left = jnp.where(col == 0, 0.0, pltpu.roll(left, 1, 1))
    right = jnp.where(col == wcol - 1, 0.0, pltpu.roll(right, wcol - 1, 1))
    return (left + mid + right) * (1.0 / math.sqrt(9 * C))


def taps_of(kernel_ref):
    def taps(lhs, kx):
        rhs = jnp.concatenate([kernel_ref[0, ky, kx] for ky in range(3)], axis=0)
        return jnp.dot(lhs, rhs, preferred_element_type=F32)

    return taps


def flipped_taps_of(kernel_ref):
    def taps(lhs, kx):
        rhs = jnp.concatenate([kernel_ref[0, 2 - ky, 2 - kx] for ky in range(3)], axis=1)
        return lax.dot_general(lhs, rhs, NT, preferred_element_type=F32)

    return taps


def chunks(count):
    return [(at, min(2, count - at)) for at in range(0, count, 2)]


def silu_rows(maps, kernel_ref, count, out_ref):
    for at, size in chunks(count):
        pre = conv_rows(maps, at, size, taps_of(kernel_ref))
        out_ref[pl.ds(at, size)] = (pre / (1.0 + jnp.exp(-pre))).astype(BF16)


def slope_rows(maps, start, kernel_ref, grads, count, dz3, to):
    for at, size in chunks(count):
        back = conv_rows(maps, start + at, size, taps_of(kernel_ref))
        sig = 1.0 / (1.0 + jnp.exp(-back))
        dz = grads[pl.ds(at, size)].astype(F32) * (sig * (1.0 + back * (1.0 - sig)))
        wcol = dz.shape[1]
        col = lax.broadcasted_iota(jnp.int32, dz.shape, 1)
        row = pl.ds(to + at, size)
        dz3[row, :, 0:C] = jnp.where(col == 0, 0.0, pltpu.roll(dz, 1, 1)).astype(BF16)
        dz3[row, :, C : 2 * C] = dz.astype(BF16)
        dz3[row, :, 2 * C :] = jnp.where(
            col == wcol - 1, 0.0, pltpu.roll(dz, wcol - 1, 1)
        ).astype(BF16)


class Middle:
    def __init__(self, dz3):
        self.dz3 = dz3

    def __getitem__(self, rows):
        return self.dz3[rows, :, C : 2 * C]


def in_grad_rows(dz3, kernel_ref, count, out_ref):
    for at, size in chunks(count):
        dx = conv_rows(Middle(dz3), at, size, flipped_taps_of(kernel_ref))
        out_ref[pl.ds(at, size)] = dx.astype(BF16)


def kernel_grad(maps, start, dz3, dz_start, rows, ky):
    wcol = maps.shape[1]
    lhs = maps[pl.ds(start + ky, rows)].reshape(rows * wcol, C)
    rhs = dz3[pl.ds(dz_start, rows)].reshape(rows * wcol, 3 * C)
    grad = lax.dot_general(lhs, rhs, TN, preferred_element_type=F32) * (1.0 / math.sqrt(9 * C))
    return [grad[:, (2 - kx) * C : (3 - kx) * C] for kx in range(3)]


def zero_row(ref, at):
    ref[pl.ds(at, 1)] = jnp.zeros((1,) + ref.shape[1:], ref.dtype)


def put(ref, at, value):
    ref[pl.ds(at, value.shape[0])] = value


def put_second_map(ref, at, slots, x_in, stash):
    same = slots[0, 0] == slots[1, 0]

    @pl.when(same)
    def _():
        put(ref, at, x_in[0])

    @pl.when(jnp.logical_not(same))
    def _():
        put(ref, at, stash[0, slots[1, 0]])


def edge(rows, count, me):
    return pl.ds((1 - me) * (rows - count), count)


def inner(rows, count, me):
    return pl.ds(me * (rows - count), count)


def run_copies(copies, sems):
    started = [pltpu.make_async_copy(a, b, sems.at[i]) for i, (a, b) in enumerate(copies)]
    for copy in started:
        copy.start()
    for copy in started:
        copy.wait()


def pack_first(slots, x_in, stash, grad, next_in, next_g, halo, edges, sems):
    me = lax.axis_index("band")
    pos = lax.axis_index("segment")
    rows = x_in.shape[1]
    turn = jnp.maximum(pos - (lax.axis_size("segment") - rows), 0)
    run_copies(
        [
            (x_in.at[0, edge(rows, 2, me)], halo.at[pl.ds(0, 2)]),
            (stash.at[0, slots[0, 0], edge(rows, 3, me)], edges.at[pl.ds(0, 3)]),
            (grad.at[0, edge(rows, 2, me)], edges.at[pl.ds(3, 2)]),
        ],
        sems,
    )

    @pl.when(pos == 0)
    def _():
        run_copies([(next_in.at[edge(rows, 1, me)], halo.at[pl.ds(2, 1)])], sems)

    @pl.when(pos != 0)
    def _():
        run_copies([(next_g.at[pl.ds(turn, 1)], halo.at[pl.ds(2, 1)])], sems)


def pack_second(slots, x_in, stash, grad, rest, edges2, rest2, sems):
    me = lax.axis_index("band")
    rows = x_in.shape[1]
    copies = [
        (stash.at[0, slots[0, 0], inner(rows, rows - 3, me)], rest.at[pl.ds(0, rows - 3)]),
        (grad.at[0, inner(rows, rows - 2, me)], rest.at[pl.ds(rows - 3, rows - 2)]),
    ]
    same = slots[0, 0] == slots[1, 0]

    @pl.when(same)
    def _():
        run_copies(
            copies
            + [
                (x_in.at[0, edge(rows, 2, me)], edges2),
                (x_in.at[0, inner(rows, rows - 2, me)], rest2),
            ],
            sems,
        )

    @pl.when(jnp.logical_not(same))
    def _():
        run_copies(
            copies
            + [
                (stash.at[0, slots[1, 0], edge(rows, 2, me)], edges2),
                (stash.at[0, slots[1, 0], inner(rows, rows - 2, me)], rest2),
            ],
            sems,
        )


def forward_one(x_in, halo, w_now, y1, maps):
    me = lax.axis_index("band")
    rows = x_in.shape[1]
    zero_row(maps, (rows + 2) * me)
    put(maps, 1 + me, x_in[0])
    put(maps, (rows + 1) * (1 - me), halo[0:2])
    silu_rows(maps, w_now, rows + 1, y1)


def forward_two(next_in, halo, arrived, w_one, act, maps):
    me = lax.axis_index("band")
    first = lax.axis_index("segment") == 0
    rows = next_in.shape[0]
    zero_row(maps, (rows + 1) * me)

    @pl.when(first)
    def _():
        put(maps, 1, next_in[...])
        put(maps, (rows + 1) * (1 - me), halo[2:3])

    @pl.when(jnp.logical_not(first))
    def _():
        put(maps, 1 - me, arrived[...])

    silu_rows(maps, w_one, rows, act.at[0])


def backward_one(slots, stash, grad, edges, w_old, dx, own_kgrad, dz3_edge, maps, grads, dz3):
    me = lax.axis_index("band")
    rows = stash.shape[2]
    zero_row(maps, (rows + 3) * me)
    put(maps, 1 + 2 * me, stash[0, slots[0, 0]])
    put(maps, (rows + 1) * (1 - me), edges[0:3])
    put(grads, 2 * me, grad[0])
    put(grads, rows * (1 - me), edges[3:5])
    zero_row(dz3, (rows + 2) * me)
    slope_rows(maps, 0, w_old, grads, rows + 2, dz3, 1 - me)
    in_grad_rows(dz3, w_old, rows + 1, dx)
    dz3_edge[...] = dz3[pl.ds((rows + 1) * (1 - me), 2)]
    for ky in range(3):
        taps = kernel_grad(maps, 2 * me, dz3, 1 + me, rows, ky)
        for kx in range(3):
            own_kgrad[ky, kx] = taps[kx]


def backward_one_rest(slots, stash, edges, rest, dz3_edge, w_old, dx, maps, dz3):
    me = lax.axis_index("band")
    rows = stash.shape[2]
    zero_row(maps, (rows + 1) * (1 - me))
    put(maps, (rows + 1) * me, stash[0, slots[0, 0], edge(rows, 1, me)])
    put(maps, 1 + (rows - 3) * me, edges[0:3])
    put(maps, 4 - 3 * me, rest[0 : rows - 3])
    zero_row(dz3, rows * (1 - me))
    put(dz3, (rows - 1) * me, dz3_edge[...])
    slope_rows(
        maps, 2 * (1 - me), w_old, rest.at[pl.ds(rows - 3, rows - 2)], rows - 2, dz3, 2 - me
    )
    in_grad_rows(dz3, w_old, rows - 1, dx)


def update_one(maps, dz3, own_kgrad, moment, w_now, m_one, w_one):
    me = lax.axis_index("band")
    rows = maps.shape[0] - 2
    for ky in range(3):
        taps = kernel_grad(maps, 0, dz3, me, rows, ky)
        for kx in range(3):
            fresh = 0.9 * moment[0, ky, kx] + (own_kgrad[ky, kx] + taps[kx])
            m_one[ky, kx] = fresh
            w_one[0, ky, kx] = (w_now[0, ky, kx].astype(F32) - 0.05 * fresh).astype(BF16)


def backward_two(
    slots, x_in, stash, edges2, returned, next_g, next_g_other, w_now,
    dx, own_kgrad, dz3_edge, maps, grads, dz3,
):
    me = lax.axis_index("band")
    last = lax.axis_index("segment") == lax.axis_size("segment") - 1
    rows = stash.shape[2]
    zero_row(maps, (rows + 2) * me)
    put_second_map(maps, 1 + me, slots, x_in, stash)
    put(maps, (rows + 1) * (1 - me), edges2[...])

    @pl.when(last)
    def _():
        put(grads, me, next_g[...])
        put(grads, rows * (1 - me), next_g_other[pl.ds((rows - 1) * me, 1)])

    @pl.when(jnp.logical_not(last))
    def _():
        put(grads, 0, returned[...])

    zero_row(dz3, (rows + 1) * me)
    slope_rows(maps, 0, w_now, grads, rows + 1, dz3, 1 - me)
    in_grad_rows(dz3, w_now, rows, dx.at[0])
    dz3_edge[...] = dz3[pl.ds((rows + 1) * (1 - me), 1)]
    for ky in range(3):
        taps = kernel_grad(maps, me, dz3, 1, rows, ky)
        for kx in range(3):
            own_kgrad[ky, kx] = taps[kx]


def backward_two_rest(
    slots, x_in, stash, edges2, rest2, dz3_edge, returned, next_g_other, w_now,
    own_kgrad, m_one, w_one, m_out, w_out, maps, own, grads, dz3, m_two, w_two, sems,
):
    me = lax.axis_index("band")
    last = lax.axis_index("segment") == lax.axis_size("segment") - 1
    rows = stash.shape[2]
    zero_row(maps, (rows + 1) * (1 - me))
    put_second_map(own, 0, slots, x_in, stash)
    put(maps, (rows + 1) * me, own[edge(rows, 1, me)])
    put(maps, 1 + (rows - 2) * me, edges2[...])
    put(maps, 3 - 2 * me, rest2[...])

    @pl.when(last)
    def _():
        put(grads, 0, next_g_other[pl.ds(1 - me, rows - 1)])

    @pl.when(jnp.logical_not(last))
    def _():
        put(grads, 0, returned[...])

    put(dz3, (rows - 1) * me, dz3_edge[...])
    slope_rows(maps, 1 - me, w_now, grads, rows - 1, dz3, 1 - me)
    copies = []
    for ky in range(3):
        taps = kernel_grad(maps, 0, dz3, 0, rows, ky)
        for kx in range(3):
            fresh = 0.9 * m_one[ky, kx] + (own_kgrad[ky, kx] + taps[kx])
            m_two[ky, kx] = fresh
            w_two[ky, kx] = (w_one[0, ky, kx].astype(F32) - 0.05 * fresh).astype(BF16)
        for at, (source, target) in enumerate(((m_two, m_out), (w_two, w_out))):
            copy = pltpu.make_async_copy(source.at[ky], target.at[0, ky], sems.at[2 * ky + at])
            copy.start()
            copies.append(copy)
    for copy in copies:
        copy.wait()


def gathered_at_last(row, rows):
    first = lax.axis_size("segment") - rows
    width = 1
    while width < rows:
        pairs = [
            (first + at + width - 1, first + at + 2 * width - 1)
            for at in range(0, rows, 2 * width)
        ]
        row = jnp.concatenate([lax.ppermute(row, "segment", pairs), row], axis=0)
        width *= 2
    return row


def two_band_body(
    first_input, stashed, first_grad, weight_now, weight_old, momentum, slot_plan,
    next_input, next_grad,
):
    rows, wcol = first_input.shape[1:3]
    unit = rows * wcol * 9 * C * C
    full = (3, 3, C, C)

    def some(count):
        return ((count, wcol, C), BF16)

    def map_rows(count):
        return pltpu.VMEM((count, wcol, C), BF16)

    def dz_rows(count):
        return pltpu.VMEM((count, wcol, 3 * C), BF16)

    def swapped(array):
        return lax.ppermute(array, "band", SWAP)

    halo, edges = call(
        pack_first, [some(3), some(5)], [SMEM] + anywhere(5), anywhere(2),
        [pltpu.SemaphoreType.DMA((3,))], 0,
    )(slot_plan, first_input, stashed, first_grad, next_input, next_grad)
    halo = swapped(halo)
    edges = swapped(edges)
    rest, edges2, rest2 = call(
        pack_second, [some(2 * rows - 5), some(2), some(rows - 2)], [SMEM] + anywhere(3),
        anywhere(3), [pltpu.SemaphoreType.DMA((4,))], 0,
    )(slot_plan, first_input, stashed, first_grad)
    rest = swapped(rest)
    edges2 = swapped(edges2)
    rest2 = swapped(rest2)
    next_grad_other = gathered_at_last(halo[2:3], rows)

    (y1,) = call(
        forward_one, [some(rows + 1)], vmem(3), vmem(1), [map_rows(rows + 3)], unit
    )(first_input, halo, weight_now)
    arrived = passed_along(y1, "segment", 1)

    dx_a, own_kgrad, dz3_edge = call(
        backward_one, [some(rows + 1), (full, F32), ((2, wcol, 3 * C), BF16)],
        [SMEM] + vmem(4), vmem(3),
        [map_rows(rows + 4), map_rows(rows + 2), dz_rows(rows + 3)], 3 * unit,
    )(slot_plan, stashed, first_grad, edges, weight_old)
    returned_a = passed_along(dx_a, "segment", -1)

    dx_b, maps, dz3 = call(
        backward_one_rest,
        [some(rows - 1), some(rows + 2), ((rows + 1, wcol, 3 * C), BF16)],
        [SMEM] + vmem(5), vmem(3), [], 2 * unit,
    )(slot_plan, stashed, edges, rest, dz3_edge, weight_old)
    returned_b = passed_along(dx_b, "segment", -1)

    m_one, w_one = call(
        update_one, [(full, F32), ((1,) + full, BF16)], vmem(5), vmem(2), [], unit
    )(maps, dz3, own_kgrad, momentum, weight_now)

    dx, own_kgrad, dz3_edge = call(
        backward_two,
        [((1, rows, wcol, C), BF16), (full, F32), ((1, wcol, 3 * C), BF16)],
        [SMEM] + vmem(7), vmem(3),
        [map_rows(rows + 3), map_rows(rows + 1), dz_rows(rows + 2)], 3 * unit,
    )(slot_plan, first_input, stashed, edges2, returned_a, next_grad, next_grad_other, weight_now)

    (act,) = call(
        forward_two, [((1, rows, wcol, C), BF16)], vmem(4), vmem(1), [map_rows(rows + 2)], unit
    )(next_input, halo, arrived, w_one)

    m_two, w_two = call(
        backward_two_rest,
        [((1,) + full, F32), ((1,) + full, BF16)],
        [SMEM] + vmem(11), anywhere(2),
        [
            map_rows(rows + 2), map_rows(rows), map_rows(rows - 1), dz_rows(rows),
            pltpu.VMEM(full, F32), pltpu.VMEM(full, BF16), pltpu.SemaphoreType.DMA((6,)),
        ],
        2 * unit,
    )(
        slot_plan, first_input, stashed, edges2, rest2, dz3_edge, returned_b, next_grad_other,
        weight_now, own_kgrad, m_one, w_one,
    )
    return act, dx, w_two, w_one, m_two


def fits_two_bands(mesh):
    return mesh.shape["band"] == 2 and mesh.shape["segment"] >= 8


def solution(mesh):
    placed = (
        P("segment", "band", None, None),
        P("segment", None, "band", None, None),
        P("segment", "band", None, None),
        P("segment", None, None, None, None),
        P("segment", None, None, None, None),
        P("segment", None, None, None, None),
        P(None, "segment"),
        P("band", None, None),
        P("band", None, None),
    )
    return jax.shard_map(
        two_band_body if fits_two_bands(mesh) else body,
        mesh=mesh,
        in_specs=placed,
        out_specs=(
            P("segment", "band", None, None),
            P("segment", "band", None, None),
            P("segment", None, None, None, None),
            P("segment", None, None, None, None),
            P("segment", None, None, None, None),
        ),
        check_vma=False,
    )
```

```python
import math

import jax
import jax.numpy as jnp
from jax import lax
from jax.experimental import pallas as pl
from jax.experimental.pallas import tpu as pltpu
from jax.sharding import PartitionSpec as P

C = 256


def padded_2(block, sides, width):
    for axis, dim in sides:
        count = lax.axis_size(axis)
        forward = [(i, i + 1) for i in range(count - 1)]
        backward = [(target, source) for source, target in forward]
        low = lax.ppermute(
            lax.slice_in_dim(block, block.shape[dim] - width, None, axis=dim), axis, forward
        )
        high = lax.ppermute(lax.slice_in_dim(block, 0, width, axis=dim), axis, backward)
        block = jnp.concatenate([low, block, high], axis=dim)
    return block


def passed_along(array, axis, by):
    length = lax.axis_size(axis)
    pairs = [(i, i + by) for i in range(length) if 0 <= i + by < length]
    return lax.ppermute(array, axis, pairs)


def row_patches(extended, rows):
    wcol = extended.shape[1]
    padded = jnp.pad(extended, ((0, 0), (1, 1), (0, 0)))
    taps = [padded[ky : ky + rows, kx : kx + wcol, :] for ky in range(3) for kx in range(3)]
    return jnp.concatenate(taps, axis=2).reshape(rows * wcol, -1)


def silu_slope(value):
    sig = jax.nn.sigmoid(value)
    return sig * (1.0 + value * (1.0 - sig))


def forward_part(x_in, flat_now, factor):
    rows, wcol = (x_in.shape[0], x_in.shape[1])
    ext = padded_2(x_in, (("band", 0),), 1)
    pre = jnp.dot(row_patches(ext, rows), flat_now, preferred_element_type=jnp.float32) * factor
    return jax.nn.silu(pre).astype(jnp.bfloat16).reshape(rows, wcol, C)


def backward_part(chosen, grad, w_old, factor):
    rows, wcol = (chosen.shape[0], chosen.shape[1])
    flat_old = w_old.reshape(9 * C, C)
    flip_old = w_old[::-1, ::-1].transpose(0, 1, 3, 2).reshape(9 * C, C)
    ext = padded_2(chosen, (("band", 0),), 1)
    patches = row_patches(ext, rows)
    back = jnp.dot(patches, flat_old, preferred_element_type=jnp.float32) * factor
    slope_grad = (grad.reshape(-1, C) * silu_slope(back)).astype(jnp.bfloat16)
    slope_ext = padded_2(slope_grad.reshape(rows, wcol, C), (("band", 0),), 1)
    kgrad = (
        lax.dot_general(
            patches, slope_grad, (((0,), (0,)), ((), ())), preferred_element_type=jnp.float32
        )
        * factor
    )
    in_grad = (
        jnp.dot(row_patches(slope_ext, rows), flip_old, preferred_element_type=jnp.float32) * factor
    )
    return (in_grad.astype(jnp.bfloat16).reshape(rows, wcol, C), kgrad)


def update_part(kgrad, w_now, moment):
    flat_now = w_now.reshape(9 * C, C).astype(jnp.float32)
    total = lax.psum(kgrad.astype(jnp.bfloat16), "band").astype(jnp.float32)
    new_moment = 0.9 * moment + total
    new_flat = (flat_now - 0.05 * new_moment).astype(jnp.bfloat16)
    return (new_flat.reshape(3, 3, C, C), new_moment)


def body(
    first_input,
    stashed,
    first_grad,
    weight_now,
    weight_old,
    momentum,
    slot_plan,
    next_input,
    next_grad,
):
    factor = 1.0 / math.sqrt(9 * C)
    segment_pos = lax.axis_index("segment")
    last_pos = lax.axis_size("segment") - 1
    x_in = first_input[0]
    stash = stashed[0]
    grad = first_grad[0]
    w_now = weight_now[0]
    w_old = weight_old[0]
    moment = momentum[0].reshape(9 * C, C)
    slots = slot_plan[:, 0]
    for tick in range(2):
        if tick == 1:
            arrived = passed_along(out_acts, "segment", 1)
            x_in = jnp.where(segment_pos == 0, next_input, arrived)
            returned = passed_along(in_grad, "segment", -1)
            grad = jnp.where(segment_pos == last_pos, next_grad, returned)
        out_acts = forward_part(x_in, w_now.reshape(9 * C, C), factor)
        chosen = lax.dynamic_index_in_dim(stash, slots[tick], 0, keepdims=False)
        in_grad, kgrad = backward_part(chosen, grad, w_old, factor)
        stash = lax.dynamic_update_index_in_dim(stash, x_in, slots[tick], 0)
        new_weight, moment = update_part(kgrad, w_now, moment)
        w_old = w_now
        w_now = new_weight
    return (out_acts[None], in_grad[None], w_now[None], w_old[None], moment.reshape(1, 3, 3, C, C))


SWAP = [(0, 1), (1, 0)]
BF16 = jnp.bfloat16
F32 = jnp.float32
NT = (((1,), (1,)), ((), ()))
TN = (((0,), (0,)), ((), ()))
MIB = 2**20


def vmem(count):
    return [pl.BlockSpec(memory_space=pltpu.VMEM)] * count


def anywhere(count):
    return [pl.BlockSpec(memory_space=pl.ANY)] * count


def hbm(count):
    return [pl.BlockSpec(memory_space=pltpu.HBM)] * count


SMEM = pl.BlockSpec(memory_space=pltpu.SMEM)


def call(kernel, outs, in_specs, out_specs, scratch, limit=24):
    count = len(in_specs)

    def ordered(*refs):
        for side in range(2):

            @pl.when(lax.axis_index("band") == side)
            def _(side=side):
                kernel(side, *refs[:count], *refs[count + 1 :])

    return pl.pallas_call(
        ordered,
        name=kernel.__name__,
        out_shape=[jax.ShapeDtypeStruct(shape, kind) for shape, kind in outs],
        in_specs=in_specs + anywhere(1),
        out_specs=out_specs,
        scratch_shapes=scratch,
        compiler_params=pltpu.CompilerParams(vmem_limit_bytes=limit * MIB),
        cost_estimate=pl.CostEstimate(flops=10**10, bytes_accessed=10**8, transcendentals=0),
    )


def conv_rows(rows_of, start, count, taps):
    lhs = [rows_of[pl.ds(start + ky, count)] for ky in range(3)]
    wcol = lhs[0].shape[1]
    lhs = jnp.concatenate([part.reshape(count * wcol, C) for part in lhs], axis=1)
    left, mid, right = (
        part.reshape(count, wcol, C) for part in (taps(lhs, 0), taps(lhs, 1), taps(lhs, 2))
    )
    col = lax.broadcasted_iota(jnp.int32, mid.shape, 1)
    left = jnp.where(col == 0, 0.0, pltpu.roll(left, 1, 1))
    right = jnp.where(col == wcol - 1, 0.0, pltpu.roll(right, wcol - 1, 1))
    return (left + mid + right) * (1.0 / math.sqrt(9 * C))


def taps_of(kernel_ref):
    def taps(lhs, kx):
        rhs = jnp.concatenate([kernel_ref[0, ky, kx] for ky in range(3)], axis=0)
        return jnp.dot(lhs, rhs, preferred_element_type=F32)

    return taps


def flipped_taps_of(kernel_ref):
    def taps(lhs, kx):
        rhs = jnp.concatenate([kernel_ref[0, 2 - ky, 2 - kx] for ky in range(3)], axis=1)
        return lax.dot_general(lhs, rhs, NT, preferred_element_type=F32)

    return taps


def chunks(count):
    return [(at, min(2, count - at)) for at in range(0, count, 2)]


def silu_rows(maps, kernel_ref, count, out_ref):
    for at, size in chunks(count):
        pre = conv_rows(maps, at, size, taps_of(kernel_ref))
        out_ref[pl.ds(at, size)] = (pre / (1.0 + jnp.exp(-pre))).astype(BF16)


def slope_rows(maps, start, kernel_ref, count, store):
    for at, size in chunks(count):
        back = conv_rows(maps, start + at, size, taps_of(kernel_ref))
        sig = 1.0 / (1.0 + jnp.exp(-back))
        store(at, sig * (1.0 + back * (1.0 - sig)))


def put_dz(dz3, to, dz):
    wcol = dz.shape[1]
    col = lax.broadcasted_iota(jnp.int32, dz.shape, 1)
    row = pl.ds(to, dz.shape[0])
    dz3[row, :, 0:C] = jnp.where(col == 0, 0.0, pltpu.roll(dz, 1, 1)).astype(BF16)
    dz3[row, :, C : 2 * C] = dz.astype(BF16)
    dz3[row, :, 2 * C :] = jnp.where(
        col == wcol - 1, 0.0, pltpu.roll(dz, wcol - 1, 1)
    ).astype(BF16)


def dz_from(maps, start, kernel_ref, grads, grads_at, count, dz3, to):
    def job(at, size):
        def run():
            def store(_, slope):
                grad = grads[pl.ds(grads_at + at, size)].astype(F32)
                put_dz(dz3, to + at, grad * slope)

            slope_rows(maps, start + at, kernel_ref, size, store)

        return (to + at, size, run)

    return [job(at, size) for at, size in chunks(count)]


def dz_from_slopes(slopes, grads, grads_at, count, dz3, to):
    def job(at, size):
        def run():
            grad = grads[pl.ds(grads_at + at, size)].astype(F32)
            put_dz(dz3, to + at, grad * slopes[pl.ds(at, size)])

        return (to + at, size, run)

    return [job(at, size) for at, size in chunks(count)]


def dz_and_in_grad(jobs, there, dz3, kernel_ref, count, out_ref):
    there = set(there)
    waiting = chunks(count)
    for first, rows, run in jobs:
        run()
        there.update(range(first, first + rows))
        for at, size in list(waiting):
            if there.issuperset(range(at, at + size + 2)):
                dx = conv_rows(Middle(dz3), at, size, flipped_taps_of(kernel_ref))
                out_ref[pl.ds(at, size)] = dx.astype(BF16)
                waiting.remove((at, size))
    assert not waiting


class Middle:
    def __init__(self, dz3):
        self.dz3 = dz3

    def __getitem__(self, rows):
        return self.dz3[rows, :, C : 2 * C]


def kernel_grad(maps, start, dz3, dz_start, rows, ky):
    wcol = maps.shape[1]
    lhs = maps[pl.ds(start + ky, rows)].reshape(rows * wcol, C)
    rhs = dz3[pl.ds(dz_start, rows)].reshape(rows * wcol, 3 * C)
    grad = lax.dot_general(lhs, rhs, TN, preferred_element_type=F32) * (1.0 / math.sqrt(9 * C))
    return [grad[:, (2 - kx) * C : (3 - kx) * C] for kx in range(3)]


def zero_row(ref, at):
    ref[pl.ds(at, 1)] = jnp.zeros((1,) + ref.shape[1:], ref.dtype)


def put(ref, at, value):
    ref[pl.ds(at, value.shape[0])] = value


def put_second_map(ref, at, slots, x_in, stash):
    same = slots[0] == slots[1]

    @pl.when(same)
    def _():
        put(ref, at, x_in[0])

    @pl.when(jnp.logical_not(same))
    def _():
        put(ref, at, stash[0, slots[1]])


def edge(rows, count, me):
    return pl.ds((1 - me) * (rows - count), count)


def inner(rows, count, me):
    return pl.ds(me * (rows - count), count)


def start_copies(copies, sems, first):
    started = [
        pltpu.make_async_copy(a, b, sems.at[first + i]) for i, (a, b) in enumerate(copies)
    ]
    for copy in started:
        copy.start()
    return started


def pack(me, slots, x_in, stash, grad, next_in, next_g, edges, mark, sems):
    pos = lax.axis_index("segment")
    rows = stash.shape[2]
    turn = jnp.maximum(pos - (lax.axis_size("segment") - rows), 0)
    mark[...] = jnp.zeros_like(mark)
    row = edges.at[pl.ds(7, 1)]
    started = start_copies(
        [
            (stash.at[0, slots[0], edge(rows, 3, me)], edges.at[pl.ds(0, 3)]),
            (grad.at[0, edge(rows, 2, me)], edges.at[pl.ds(3, 2)]),
            (x_in.at[0, edge(rows, 2, me)], edges.at[pl.ds(5, 2)]),
        ],
        sems, 0,
    )

    @pl.when(pos == 0)
    def _():
        start_copies([(next_in.at[edge(rows, 1, me)], row)], sems, 3)

    @pl.when(pos != 0)
    def _():
        start_copies([(next_g.at[pl.ds(turn, 1)], row)], sems, 3)

    started.append(pltpu.make_async_copy(next_g.at[pl.ds(0, 1)], row, sems.at[3]))
    for copy in started:
        copy.wait()


def pack_rest(me, slots, x_in, stash, grad, next_in, rest, one, two, next_kept):
    rows = x_in.shape[1]
    one[...] = stash[0, slots[0]]
    put_second_map(two, 0, slots, x_in, stash)
    rest[0 : rows - 3] = one[inner(rows, rows - 3, me)]
    rest[rows - 3 : 2 * rows - 5] = grad[0, inner(rows, rows - 2, me)]
    rest[2 * rows - 5 :] = two[edge(rows, 2, me)]
    next_kept[...] = next_in[...]


def early(me, one, two, x_in, w_old, w_now, y1, slope1, slope2, maps):
    rows = x_in.shape[1]
    put(maps, 1 - me, two[...])
    zero_row(maps, rows * me)

    def keep(slopes):
        def store(at, slope):
            slopes[pl.ds(at, slope.shape[0])] = slope

        return store

    slope_rows(maps, 0, w_now, rows - 1, keep(slope2))
    put(maps, 1 - me, one[...])
    slope_rows(maps, 0, w_old, rows - 1, keep(slope1))
    put(maps, 1 - me, x_in[0])
    silu_rows(maps, w_now, rows - 1, y1)


def forward_two(me, next_in, edges, arrived, w_one, act, maps):
    first = lax.axis_index("segment") == 0
    rows = next_in.shape[0]
    zero_row(maps, (rows + 1) * me)

    @pl.when(first)
    def _():
        put(maps, 1, next_in[...])
        put(maps, (rows + 1) * (1 - me), edges[7:8])

    @pl.when(jnp.logical_not(first))
    def _():
        put(maps, 1 - me, arrived[...])

    silu_rows(maps, w_one, rows, act)


def backward_one(
    me, one, two, x_in, grad, edges, w_old, w_now, slope1, y1_far,
    dx, y1, rest2, dz3_edge, maps, dz3, border,
):
    rows = one.shape[0]
    rest2[...] = two[inner(rows, rows - 2, me)]
    put(border, 2 * me, x_in[0, edge(rows, 2, me)])
    put(border, 2 * (1 - me), edges[5:7])
    silu_rows(border, w_now, 2, y1.at[pl.ds((rows - 1) * (1 - me), 2)])
    put(y1, 2 * me, y1_far[...])
    zero_row(maps, (rows + 3) * me)
    put(maps, 1 + 2 * me, one[...])
    put(maps, (rows + 1) * (1 - me), edges[0:3])
    zero_row(dz3, (rows + 2) * me)
    own = 1 + me
    far = own + me
    near = own + (rows - 1) * (1 - me)
    other = own + rows * (1 - me) - 2 * me
    jobs = dz_from(maps, near - 1 + me, w_old, grad.at[0], (rows - 1) * (1 - me), 1, dz3, near)
    jobs += dz_from(maps, other - 1 + me, w_old, edges, 3, 2, dz3, other)
    jobs += dz_from_slopes(slope1, grad.at[0], me, rows - 1, dz3, far)
    dz_and_in_grad(jobs, [(rows + 2) * me], dz3, w_old, rows + 1, dx)
    dz3_edge[...] = dz3[pl.ds((rows + 1) * (1 - me), 2)]


def own_kernel_grad(me, maps, dz3, own_kgrad):
    rows = maps.shape[0] - 4
    for ky in range(3):
        taps = kernel_grad(maps, 2 * me, dz3, 1 + me, rows, ky)
        for kx in range(3):
            own_kgrad[ky, kx] = taps[kx]


def backward_one_rest(me, one, edges, rest, dz3_edge, w_old, dx, maps, dz3):
    rows = one.shape[0]
    zero_row(maps, (rows + 1) * (1 - me))
    put(maps, (rows + 1) * me, one[edge(rows, 1, me)])
    put(maps, 1 + (rows - 3) * me, edges[0:3])
    put(maps, 4 - 3 * me, rest[0 : rows - 3])
    zero_row(dz3, rows * (1 - me))
    put(dz3, (rows - 1) * me, dz3_edge[...])
    jobs = dz_from(maps, 2 * (1 - me), w_old, rest, rows - 3, rows - 2, dz3, 2 - me)
    there = [rows * (1 - me), (rows - 1) * me, (rows - 1) * me + 1]
    dz_and_in_grad(jobs, there, dz3, w_old, rows - 1, dx)


def update_one(me, maps, dz3, own_kgrad, moment, w_now, m_one, w_one):
    rows = maps.shape[0] - 2
    for ky in range(3):
        taps = kernel_grad(maps, 0, dz3, me, rows, ky)
        for kx in range(3):
            fresh = 0.9 * moment[0, ky, kx] + (own_kgrad[ky, kx] + taps[kx])
            m_one[ky, kx] = fresh
            w_one[0, ky, kx] = (w_now[0, ky, kx].astype(F32) - 0.05 * fresh).astype(BF16)


def backward_two(
    me, two, rest, returned, next_g, next_g_other, w_now, slope2,
    dx, own_kgrad, dz3_edge, maps, grads, dz3,
):
    last = lax.axis_index("segment") == lax.axis_size("segment") - 1
    rows = two.shape[0]
    zero_row(maps, (rows + 2) * me)
    put(maps, 1 + me, two[...])
    put(maps, (rows + 1) * (1 - me), rest[2 * rows - 5 :])

    @pl.when(last)
    def _():
        put(grads, me, next_g[...])
        put(grads, rows * (1 - me), next_g_other[pl.ds((rows - 1) * me, 1)])

    @pl.when(jnp.logical_not(last))
    def _():
        put(grads, 0, returned[...])

    zero_row(dz3, (rows + 1) * me)
    near = (rows - 1) * (1 - me)
    jobs = dz_from(maps, near, w_now, grads, near, 2, dz3, near + 1 - me)
    jobs += dz_from_slopes(slope2, grads, 2 * me, rows - 1, dz3, 1 + me)
    dz_and_in_grad(jobs, [(rows + 1) * me], dz3, w_now, rows, dx)
    dz3_edge[...] = dz3[pl.ds((rows + 1) * (1 - me), 1)]
    for ky in range(3):
        taps = kernel_grad(maps, me, dz3, 1, rows, ky)
        for kx in range(3):
            own_kgrad[ky, kx] = taps[kx]


def finish(
    me, two, rest, rest2, dz3_edge, returned, next_g_other, w_now,
    own_kgrad, m_one, w_one, next_in, edges, arrived, dx,
    act_out, dx_out, m_out, w_out, w_one_out, maps, grads, dz3, act, m_two, w_two, sems,
):
    last = lax.axis_index("segment") == lax.axis_size("segment") - 1
    rows = next_in.shape[0]
    copies = start_copies([(w_one, w_one_out), (dx, dx_out.at[0])], sems, 7)
    forward_two(me, next_in, edges, arrived, w_one, act, maps)
    copies += start_copies([(act, act_out.at[0])], sems, 6)
    zero_row(maps, (rows + 1) * (1 - me))
    put(maps, (rows + 1) * me, two[edge(rows, 1, me)])
    put(maps, 1 + (rows - 2) * me, rest[2 * rows - 5 :])
    put(maps, 3 - 2 * me, rest2[...])

    @pl.when(last)
    def _():
        put(grads, 0, next_g_other[pl.ds(1 - me, rows - 1)])

    @pl.when(jnp.logical_not(last))
    def _():
        put(grads, 0, returned[...])

    put(dz3, (rows - 1) * me, dz3_edge[...])
    for _, _, run in dz_from(maps, 1 - me, w_now, grads, 0, rows - 1, dz3, 1 - me):
        run()
    for ky in range(3):
        taps = kernel_grad(maps, 0, dz3, 0, rows, ky)
        for kx in range(3):
            fresh = 0.9 * m_one[ky, kx] + (own_kgrad[ky, kx] + taps[kx])
            m_two[ky, kx] = fresh
            w_two[ky, kx] = (w_one[0, ky, kx].astype(F32) - 0.05 * fresh).astype(BF16)
        copies += start_copies(
            [(m_two.at[ky], m_out.at[0, ky]), (w_two.at[ky], w_out.at[0, ky])], sems, 2 * ky
        )
    for copy in copies:
        copy.wait()


def gathered_at_last(row, rows):
    first = lax.axis_size("segment") - rows
    width = 1
    while width < rows:
        pairs = [
            (first + at + width - 1, first + at + 2 * width - 1)
            for at in range(0, rows, 2 * width)
        ]
        row = jnp.concatenate([lax.ppermute(row, "segment", pairs), row], axis=0)
        width *= 2
    return row


def two_band_body(
    first_input, stashed, first_grad, weight_now, weight_old, momentum, slot_plan,
    next_input, next_grad,
):
    rows, wcol = first_input.shape[1:3]
    unit = rows * wcol * 9 * C * C
    full = (3, 3, C, C)

    def some(count):
        return ((count, wcol, C), BF16)

    def map_rows(count):
        return pltpu.VMEM((count, wcol, C), BF16)

    def dz_rows(count):
        return pltpu.VMEM((count, wcol, 3 * C), BF16)

    def swapped(array):
        return lax.ppermute(array, "band", SWAP)

    slots = slot_plan.reshape(2)
    edges, mark = call(
        pack, [some(8), ((8, 128), F32)], [SMEM] + hbm(5), vmem(2),
        [pltpu.SemaphoreType.DMA((4,))], 56,
    )(slots, first_input, stashed, first_grad, next_input, next_grad, slots)
    edges = swapped(edges)
    rest, one, two, next_kept = call(
        pack_rest, [some(2 * rows - 3)] + [some(rows)] * 3, [SMEM] + vmem(4), vmem(4), [],
    )(slots, first_input, stashed, first_grad, next_input, mark)
    rest = swapped(rest)

    slopes = ((rows - 1, wcol, C), F32)
    y1_far, slope1, slope2 = call(
        early, [some(rows - 1), slopes, slopes], vmem(5), vmem(3), [map_rows(rows + 1)],
    )(one, two, first_input, weight_old, weight_now, two)

    dx_near, y1, rest2, dz3_edge, maps, dz3 = call(
        backward_one,
        [
            some(rows + 1), some(rows + 1), some(rows - 2), ((2, wcol, 3 * C), BF16), some(rows + 4),
            ((rows + 3, wcol, 3 * C), BF16),
        ],
        vmem(9), vmem(6), [map_rows(4)],
    )(one, two, first_input, first_grad, edges, weight_old, weight_now, slope1, y1_far, two)
    returned_near = passed_along(dx_near, "segment", -1)
    x2 = passed_along(y1, "segment", 1)
    rest2 = swapped(rest2)
    next_grad_other = gathered_at_last(edges[7:8], rows)
    (own_kgrad,) = call(own_kernel_grad, [(full, F32)], vmem(2), vmem(1), [])(maps, dz3, dx_near)

    dx_far, maps, dz3 = call(
        backward_one_rest,
        [some(rows - 1), some(rows + 2), ((rows + 1, wcol, 3 * C), BF16)],
        vmem(5), vmem(3), [],
    )(one, edges, rest, dz3_edge, weight_old, own_kgrad)
    returned_far = passed_along(dx_far, "segment", -1)

    m_one, w_one = call(
        update_one, [(full, F32), ((1,) + full, BF16)], vmem(5), vmem(2), [],
    )(maps, dz3, own_kgrad, momentum, weight_now, dx_far)

    dx, own_kgrad, dz3_edge = call(
        backward_two,
        [some(rows), (full, F32), ((1, wcol, 3 * C), BF16)],
        vmem(7), vmem(3),
        [map_rows(rows + 3), map_rows(rows + 1), dz_rows(rows + 2)],
    )(
        two, rest, returned_near, next_grad, next_grad_other,
        weight_now, slope2, m_one,
    )

    act, dx, m_two, w_two, w_one_out = call(
        finish,
        [((1, rows, wcol, C), BF16)] * 2 + [((1,) + full, F32)] + [((1,) + full, BF16)] * 2,
        vmem(14), hbm(5),
        [
            map_rows(rows + 2), map_rows(rows - 1), dz_rows(rows),
            map_rows(rows), pltpu.VMEM(full, F32), pltpu.VMEM(full, BF16),
            pltpu.SemaphoreType.DMA((9,)),
        ],
    )(
        two, rest, rest2, dz3_edge, returned_far, next_grad_other,
        weight_now, own_kgrad, m_one, w_one, next_kept, edges, x2, dx, dz3_edge,
    )
    return act, dx, w_two, w_one_out, m_two


def fits_two_bands(mesh):
    return mesh.shape["band"] == 2 and mesh.shape["segment"] >= 8


def solution(mesh):
    placed = (
        P("segment", "band", None, None),
        P("segment", None, "band", None, None),
        P("segment", "band", None, None),
        P("segment", None, None, None, None),
        P("segment", None, None, None, None),
        P("segment", None, None, None, None),
        P(None, "segment"),
        P("band", None, None),
        P("band", None, None),
    )
    return jax.shard_map(
        two_band_body if fits_two_bands(mesh) else body,
        mesh=mesh,
        in_specs=placed,
        out_specs=(
            P("segment", "band", None, None),
            P("segment", "band", None, None),
            P("segment", None, None, None, None),
            P("segment", None, None, None, None),
            P("segment", None, None, None, None),
        ),
        check_vma=False,
    )
```

```python
import functools
import math

import jax
import jax.numpy as jnp
from jax import lax
from jax.experimental import pallas as pl
from jax.experimental.pallas import tpu as pltpu
from jax.sharding import PartitionSpec as P

C = 256


def padded_2(block, sides, width):
    for axis, dim in sides:
        count = lax.axis_size(axis)
        forward = [(i, i + 1) for i in range(count - 1)]
        backward = [(target, source) for source, target in forward]
        low = lax.ppermute(
            lax.slice_in_dim(block, block.shape[dim] - width, None, axis=dim), axis, forward
        )
        high = lax.ppermute(lax.slice_in_dim(block, 0, width, axis=dim), axis, backward)
        block = jnp.concatenate([low, block, high], axis=dim)
    return block


def passed_along(array, axis, by):
    length = lax.axis_size(axis)
    pairs = [(i, i + by) for i in range(length) if 0 <= i + by < length]
    return lax.ppermute(array, axis, pairs)


def row_patches(extended, rows):
    wcol = extended.shape[1]
    padded = jnp.pad(extended, ((0, 0), (1, 1), (0, 0)))
    taps = [padded[ky : ky + rows, kx : kx + wcol, :] for ky in range(3) for kx in range(3)]
    return jnp.concatenate(taps, axis=2).reshape(rows * wcol, -1)


def silu_slope(value):
    sig = jax.nn.sigmoid(value)
    return sig * (1.0 + value * (1.0 - sig))


def forward_part(x_in, flat_now, factor):
    rows, wcol = (x_in.shape[0], x_in.shape[1])
    ext = padded_2(x_in, (("band", 0),), 1)
    pre = jnp.dot(row_patches(ext, rows), flat_now, preferred_element_type=jnp.float32) * factor
    return jax.nn.silu(pre).astype(jnp.bfloat16).reshape(rows, wcol, C)


def backward_part(chosen, grad, w_old, factor):
    rows, wcol = (chosen.shape[0], chosen.shape[1])
    flat_old = w_old.reshape(9 * C, C)
    flip_old = w_old[::-1, ::-1].transpose(0, 1, 3, 2).reshape(9 * C, C)
    ext = padded_2(chosen, (("band", 0),), 1)
    patches = row_patches(ext, rows)
    back = jnp.dot(patches, flat_old, preferred_element_type=jnp.float32) * factor
    slope_grad = (grad.reshape(-1, C) * silu_slope(back)).astype(jnp.bfloat16)
    slope_ext = padded_2(slope_grad.reshape(rows, wcol, C), (("band", 0),), 1)
    kgrad = (
        lax.dot_general(
            patches, slope_grad, (((0,), (0,)), ((), ())), preferred_element_type=jnp.float32
        )
        * factor
    )
    in_grad = (
        jnp.dot(row_patches(slope_ext, rows), flip_old, preferred_element_type=jnp.float32) * factor
    )
    return (in_grad.astype(jnp.bfloat16).reshape(rows, wcol, C), kgrad)


def update_part(kgrad, w_now, moment):
    flat_now = w_now.reshape(9 * C, C).astype(jnp.float32)
    total = lax.psum(kgrad.astype(jnp.bfloat16), "band").astype(jnp.float32)
    new_moment = 0.9 * moment + total
    new_flat = (flat_now - 0.05 * new_moment).astype(jnp.bfloat16)
    return (new_flat.reshape(3, 3, C, C), new_moment)


def body(
    first_input,
    stashed,
    first_grad,
    weight_now,
    weight_old,
    momentum,
    slot_plan,
    next_input,
    next_grad,
):
    factor = 1.0 / math.sqrt(9 * C)
    segment_pos = lax.axis_index("segment")
    last_pos = lax.axis_size("segment") - 1
    x_in = first_input[0]
    stash = stashed[0]
    grad = first_grad[0]
    w_now = weight_now[0]
    w_old = weight_old[0]
    moment = momentum[0].reshape(9 * C, C)
    slots = slot_plan[:, 0]
    for tick in range(2):
        if tick == 1:
            arrived = passed_along(out_acts, "segment", 1)
            x_in = jnp.where(segment_pos == 0, next_input, arrived)
            returned = passed_along(in_grad, "segment", -1)
            grad = jnp.where(segment_pos == last_pos, next_grad, returned)
        out_acts = forward_part(x_in, w_now.reshape(9 * C, C), factor)
        chosen = lax.dynamic_index_in_dim(stash, slots[tick], 0, keepdims=False)
        in_grad, kgrad = backward_part(chosen, grad, w_old, factor)
        stash = lax.dynamic_update_index_in_dim(stash, x_in, slots[tick], 0)
        new_weight, moment = update_part(kgrad, w_now, moment)
        w_old = w_now
        w_now = new_weight
    return (out_acts[None], in_grad[None], w_now[None], w_old[None], moment.reshape(1, 3, 3, C, C))


SWAP = [(0, 1), (1, 0)]
BF16 = jnp.bfloat16
F32 = jnp.float32
NT = (((1,), (1,)), ((), ()))
TN = (((0,), (0,)), ((), ()))
MIB = 2**20


def vmem(count):
    return [pl.BlockSpec(memory_space=pltpu.VMEM)] * count


def anywhere(count):
    return [pl.BlockSpec(memory_space=pl.ANY)] * count


def hbm(count):
    return [pl.BlockSpec(memory_space=pltpu.HBM)] * count


SMEM = pl.BlockSpec(memory_space=pltpu.SMEM)


def call(kernel, outs, in_specs, out_specs, scratch, limit=24):
    count = len(in_specs)

    def ordered(*refs):
        kernel(lax.axis_index("band"), *refs[:count], *refs[count + 1 :])

    return pl.pallas_call(
        ordered,
        name=kernel.__name__,
        out_shape=[jax.ShapeDtypeStruct(shape, kind) for shape, kind in outs],
        in_specs=in_specs + anywhere(1),
        out_specs=out_specs,
        scratch_shapes=scratch,
        compiler_params=pltpu.CompilerParams(vmem_limit_bytes=limit * MIB),
        cost_estimate=pl.CostEstimate(flops=10**10, bytes_accessed=10**8, transcendentals=0),
    )


def conv_rows(rows_of, start, count, taps):
    lhs = [rows_of[pl.ds(start + ky, count)] for ky in range(3)]
    wcol = lhs[0].shape[1]
    lhs = jnp.concatenate([part.reshape(count * wcol, C) for part in lhs], axis=1)
    left, mid, right = (
        part.reshape(count, wcol, C) for part in (taps(lhs, 0), taps(lhs, 1), taps(lhs, 2))
    )
    col = lax.broadcasted_iota(jnp.int32, mid.shape, 1)
    left = jnp.where(col == 0, 0.0, pltpu.roll(left, 1, 1))
    right = jnp.where(col == wcol - 1, 0.0, pltpu.roll(right, wcol - 1, 1))
    return (left + mid + right) * (1.0 / math.sqrt(9 * C))


def on_either_side(me, part):
    for side in range(2):
        pl.when(me == side)(functools.partial(part, side))


def taps_of(kernel_ref):
    def taps(lhs, kx):
        rhs = jnp.concatenate([kernel_ref[0, ky, kx] for ky in range(3)], axis=0)
        return jnp.dot(lhs, rhs, preferred_element_type=F32)

    return taps


def flipped_taps_of(kernel_ref):
    def taps(lhs, kx):
        rhs = jnp.concatenate([kernel_ref[0, 2 - ky, 2 - kx] for ky in range(3)], axis=1)
        return lax.dot_general(lhs, rhs, NT, preferred_element_type=F32)

    return taps


def chunks(count):
    return [(at, min(2, count - at)) for at in range(0, count, 2)]


def silu_rows(maps, kernel_ref, count, out_ref, base=0):
    for at, size in chunks(count):
        pre = conv_rows(maps, base + at, size, taps_of(kernel_ref))
        out_ref[pl.ds(base + at, size)] = (pre / (1.0 + jnp.exp(-pre))).astype(BF16)


def slope_rows(maps, start, kernel_ref, count, store):
    for at, size in chunks(count):
        back = conv_rows(maps, start + at, size, taps_of(kernel_ref))
        sig = 1.0 / (1.0 + jnp.exp(-back))
        store(at, sig * (1.0 + back * (1.0 - sig)))


def put_dz(dz3, to, dz):
    wcol = dz.shape[1]
    col = lax.broadcasted_iota(jnp.int32, dz.shape, 1)
    row = pl.ds(to, dz.shape[0])
    dz3[row, :, 0:C] = jnp.where(col == 0, 0.0, pltpu.roll(dz, 1, 1)).astype(BF16)
    dz3[row, :, C : 2 * C] = dz.astype(BF16)
    dz3[row, :, 2 * C :] = jnp.where(
        col == wcol - 1, 0.0, pltpu.roll(dz, wcol - 1, 1)
    ).astype(BF16)


def dz_from(maps, start, kernel_ref, grads, grads_at, count, dz3, to):
    def job(at, size):
        def run():
            def store(_, slope):
                grad = grads[pl.ds(grads_at + at, size)].astype(F32)
                put_dz(dz3, to + at, grad * slope)

            slope_rows(maps, start + at, kernel_ref, size, store)

        return (to + at, size, run)

    return [job(at, size) for at, size in chunks(count)]


def dz_from_slopes(slopes, grads, grads_at, count, dz3, to):
    def job(at, size):
        def run():
            grad = grads[pl.ds(grads_at + at, size)].astype(F32)
            put_dz(dz3, to + at, grad * slopes[pl.ds(at, size)])

        return (to + at, size, run)

    return [job(at, size) for at, size in chunks(count)]


def dz_and_in_grad(jobs, there, dz3, kernel_ref, count, out_ref):
    there = set(there)
    waiting = chunks(count)
    for first, rows, run in jobs:
        run()
        there.update(range(first, first + rows))
        for at, size in list(waiting):
            if there.issuperset(range(at, at + size + 2)):
                dx = conv_rows(Middle(dz3), at, size, flipped_taps_of(kernel_ref))
                out_ref[pl.ds(at, size)] = dx.astype(BF16)
                waiting.remove((at, size))
    assert not waiting


class Middle:
    def __init__(self, dz3):
        self.dz3 = dz3

    def __getitem__(self, rows):
        return self.dz3[rows, :, C : 2 * C]


def kernel_grad(maps, start, dz3, dz_start, rows, ky):
    wcol = maps.shape[1]
    lhs = maps[pl.ds(start + ky, rows)].reshape(rows * wcol, C)
    rhs = dz3[pl.ds(dz_start, rows)].reshape(rows * wcol, 3 * C)
    grad = lax.dot_general(lhs, rhs, TN, preferred_element_type=F32) * (1.0 / math.sqrt(9 * C))
    return [grad[:, (2 - kx) * C : (3 - kx) * C] for kx in range(3)]


def zero_row(ref, at):
    ref[pl.ds(at, 1)] = jnp.zeros((1,) + ref.shape[1:], ref.dtype)


def put(ref, at, value):
    ref[pl.ds(at, value.shape[0])] = value


def put_second_map(ref, at, slots, x_in, stash):
    same = slots[0] == slots[1]

    @pl.when(same)
    def _():
        put(ref, at, x_in[0])

    @pl.when(jnp.logical_not(same))
    def _():
        put(ref, at, stash[0, slots[1]])


def edge(rows, count, me):
    return pl.ds((1 - me) * (rows - count), count)


def inner(rows, count, me):
    return pl.ds(me * (rows - count), count)


def start_copies(copies, sems, first):
    started = [
        pltpu.make_async_copy(a, b, sems.at[first + i]) for i, (a, b) in enumerate(copies)
    ]
    for copy in started:
        copy.start()
    return started


def pack(me, slots, x_in, stash, grad, edges, mark, sems):
    rows = stash.shape[2]
    mark[...] = jnp.zeros_like(mark)
    copies = start_copies(
        [
            (stash.at[0, slots[0], edge(rows, 3, me)], edges.at[pl.ds(0, 3)]),
            (grad.at[0, edge(rows, 2, me)], edges.at[pl.ds(3, 2)]),
            (x_in.at[0, edge(rows, 2, me)], edges.at[pl.ds(5, 2)]),
        ],
        sems, 0,
    )
    for copy in copies:
        copy.wait()


def pack_rest(
    me, slots, x_in, stash, grad, next_in, next_g, rest, one, two, next_kept, low, high
):
    rows = x_in.shape[1]
    one[...] = stash[0, slots[0]]
    put_second_map(two, 0, slots, x_in, stash)
    rest[0 : rows - 3] = one[inner(rows, rows - 3, me)]
    rest[rows - 3 :] = grad[0, inner(rows, rows - 2, me)]
    next_kept[...] = next_in[...]
    first = lax.axis_index("segment") == 0
    low[...] = next_g[0 : rows // 2]

    @pl.when(first)
    def _():
        high[...] = next_in[edge(rows, rows // 2, me)]

    @pl.when(jnp.logical_not(first))
    def _():
        high[...] = next_g[rows // 2 :]


def early(
    me, one, two, x_in, w_old, w_now, y1, slope1, slope2, edges2, maps_x, maps_one, maps_two,
):
    rows = x_in.shape[1]
    edges2[...] = two[edge(rows, 2, me)]
    for maps, source in ((maps_x, x_in[0]), (maps_one, one[...]), (maps_two, two[...])):
        zero_row(maps, rows * me)
        put(maps, 1 - me, source)

    def keep(slopes, base):
        def store(at, slope):
            slopes[pl.ds(base + at, slope.shape[0])] = slope

        return store

    def looped(step):
        pairs = (rows - 1) // 2
        lax.fori_loop(0, pairs, lambda at, _: step(2 * at, 2), None)
        if (rows - 1) % 2:
            step(2 * pairs, 1)

    looped(lambda at, size: slope_rows(maps_two, at, w_now, size, keep(slope2, at)))
    looped(lambda at, size: slope_rows(maps_one, at, w_old, size, keep(slope1, at)))
    looped(lambda at, size: silu_rows(maps_x, w_now, size, y1, at))


def forward_two(me, next_in, beside, arrived, w_one, act, maps):
    first = lax.axis_index("segment") == 0
    rows = next_in.shape[0]
    zero_row(maps, (rows + 1) * me)

    @pl.when(first)
    def _():
        put(maps, 1, next_in[...])
        put(maps, (rows + 1) * (1 - me), beside[pl.ds((rows // 2 - 1) * me, 1)])

    @pl.when(jnp.logical_not(first))
    def _():
        put(maps, 1 - me, arrived[...])

    silu_rows(maps, w_one, rows, act)


def backward_one(
    me, one, two, x_in, grad, edges, w_old, w_now, slope1, y1_far,
    dx, y1, rest2, dz3_edge, maps, dz3, border,
):
    rows = one.shape[0]
    rest2[...] = two[inner(rows, rows - 2, me)]
    put(border, 2 * me, x_in[0, edge(rows, 2, me)])
    put(border, 2 * (1 - me), edges[5:7])
    silu_rows(border, w_now, 2, y1.at[pl.ds((rows - 1) * (1 - me), 2)])
    put(y1, 2 * me, y1_far[...])
    zero_row(maps, (rows + 3) * me)
    put(maps, 1 + 2 * me, one[...])
    put(maps, (rows + 1) * (1 - me), edges[0:3])
    zero_row(dz3, (rows + 2) * me)

    def part(me):
        own = 1 + me
        near = own + (rows - 1) * (1 - me)
        other = own + rows * (1 - me) - 2 * me
        jobs = dz_from(maps, near - 1 + me, w_old, grad.at[0], (rows - 1) * (1 - me), 1, dz3, near)
        jobs += dz_from(maps, other - 1 + me, w_old, edges, 3, 2, dz3, other)
        jobs += dz_from_slopes(slope1, grad.at[0], me, rows - 1, dz3, own + me)
        dz_and_in_grad(jobs, [(rows + 2) * me], dz3, w_old, rows + 1, dx)

    on_either_side(me, part)
    dz3_edge[...] = dz3[pl.ds((rows + 1) * (1 - me), 2)]


def keep_kernel_grad(maps, start, dz3, dz_start, rows, out, unroll):
    def step(ky, _):
        taps = kernel_grad(maps, start, dz3, dz_start, rows, ky)
        for kx in range(3):
            out[ky, kx] = taps[kx]

    lax.fori_loop(0, 3, step, None, unroll=unroll)


def own_kernel_grad(me, maps, dz3, own_kgrad):
    rows = maps.shape[0] - 4
    keep_kernel_grad(maps, 2 * me, dz3, 1 + me, rows, own_kgrad, 1)


def backward_one_rest(
    me, one, edges, rest, dz3_edge, w_old, low, high, dx, maps, dz3, next_g_other
):
    rows = one.shape[0]
    zero_row(maps, (rows + 1) * (1 - me))
    put(next_g_other, 0, low[...])
    put(next_g_other, rows // 2, high[...])
    put(maps, (rows + 1) * me, one[edge(rows, 1, me)])
    put(maps, 1 + (rows - 3) * me, edges[0:3])
    put(maps, 4 - 3 * me, rest[0 : rows - 3])
    zero_row(dz3, rows * (1 - me))
    put(dz3, (rows - 1) * me, dz3_edge[...])

    def part(me):
        jobs = dz_from(maps, 2 * (1 - me), w_old, rest, rows - 3, rows - 2, dz3, 2 - me)
        there = [rows * (1 - me), (rows - 1) * me, (rows - 1) * me + 1]
        dz_and_in_grad(jobs, there, dz3, w_old, rows - 1, dx)

    on_either_side(me, part)


def update_one(me, maps, dz3, own_kgrad, moment, w_now, m_one, w_one):
    rows = maps.shape[0] - 2

    def step(ky, _):
        taps = kernel_grad(maps, 0, dz3, me, rows, ky)
        for kx in range(3):
            fresh = 0.9 * moment[0, ky, kx] + (own_kgrad[ky, kx] + taps[kx])
            m_one[ky, kx] = fresh
            w_one[0, ky, kx] = (w_now[0, ky, kx].astype(F32) - 0.05 * fresh).astype(BF16)

    lax.fori_loop(0, 3, step, None)


def backward_two(
    me, two, edges2, returned, next_g, next_g_other, w_now, slope2,
    dx, own_kgrad, dz3_edge, maps, grads, dz3,
):
    last = lax.axis_index("segment") == lax.axis_size("segment") - 1
    rows = two.shape[0]
    zero_row(maps, (rows + 2) * me)
    put(maps, 1 + me, two[...])
    put(maps, (rows + 1) * (1 - me), edges2[...])

    @pl.when(last)
    def _():
        put(grads, me, next_g[...])
        put(grads, rows * (1 - me), next_g_other[pl.ds((rows - 1) * me, 1)])

    @pl.when(jnp.logical_not(last))
    def _():
        put(grads, 0, returned[...])

    zero_row(dz3, (rows + 1) * me)

    def part(me):
        near = (rows - 1) * (1 - me)
        jobs = dz_from(maps, near, w_now, grads, near, 2, dz3, near + 1 - me)
        jobs += dz_from_slopes(slope2, grads, 2 * me, rows - 1, dz3, 1 + me)
        dz_and_in_grad(jobs, [(rows + 1) * me], dz3, w_now, rows, dx)

    on_either_side(me, part)
    dz3_edge[...] = dz3[pl.ds((rows + 1) * (1 - me), 1)]
    keep_kernel_grad(maps, me, dz3, 1, rows, own_kgrad, 3)


def finish(
    me, two, edges2, rest2, dz3_edge, returned, next_g_other, w_now,
    own_kgrad, m_one, w_one, dx, act,
    act_out, dx_out, m_out, w_out, w_one_out, maps, grads, dz3, m_two, w_two, sems,
):
    last = lax.axis_index("segment") == lax.axis_size("segment") - 1
    rows = two.shape[0]
    copies = start_copies(
        [(act, act_out.at[0]), (w_one, w_one_out), (dx, dx_out.at[0])], sems, 6
    )
    zero_row(maps, (rows + 1) * (1 - me))
    put(maps, (rows + 1) * me, two[edge(rows, 1, me)])
    put(maps, 1 + (rows - 2) * me, edges2[...])
    put(maps, 3 - 2 * me, rest2[...])

    @pl.when(last)
    def _():
        put(grads, 0, next_g_other[pl.ds(1 - me, rows - 1)])

    @pl.when(jnp.logical_not(last))
    def _():
        put(grads, 0, returned[...])

    put(dz3, (rows - 1) * me, dz3_edge[...])
    for _, _, run in dz_from(maps, 1 - me, w_now, grads, 0, rows - 1, dz3, 1 - me):
        run()

    def outputs(ky):
        return [(m_two.at[ky], m_out.at[0, ky]), (w_two.at[ky], w_out.at[0, ky])]

    def step(ky, _):
        taps = kernel_grad(maps, 0, dz3, 0, rows, ky)
        for kx in range(3):
            fresh = 0.9 * m_one[ky, kx] + (own_kgrad[ky, kx] + taps[kx])
            m_two[ky, kx] = fresh
            w_two[ky, kx] = (w_one[0, ky, kx].astype(F32) - 0.05 * fresh).astype(BF16)
        copies.extend(start_copies(outputs(ky), sems, 2 * ky))

    for ky in range(3):
        step(ky, None)
    for copy in copies:
        copy.wait()


def two_band_body(
    first_input, stashed, first_grad, weight_now, weight_old, momentum, slot_plan,
    next_input, next_grad,
):
    rows, wcol = first_input.shape[1:3]
    unit = rows * wcol * 9 * C * C
    full = (3, 3, C, C)

    def some(count):
        return ((count, wcol, C), BF16)

    def map_rows(count):
        return pltpu.VMEM((count, wcol, C), BF16)

    def dz_rows(count):
        return pltpu.VMEM((count, wcol, 3 * C), BF16)

    def swapped(array):
        return lax.ppermute(array, "band", SWAP)

    slots = slot_plan.reshape(2)
    edges, mark = call(
        pack, [some(7), ((8, 128), F32)], [SMEM] + hbm(3), vmem(2),
        [pltpu.SemaphoreType.DMA((3,))], 56,
    )(slots, first_input, stashed, first_grad, slots)
    edges = swapped(edges)

    rest, one, two, next_kept, low, high = call(
        pack_rest, [some(2 * rows - 5)] + [some(rows)] * 3 + [some(rows // 2)] * 2,
        [SMEM] + vmem(5), vmem(6), [],
    )(slots, first_input, stashed, first_grad, next_input, next_grad, mark)
    rest = swapped(rest)

    def to_last(array, source, pairs=()):
        last = lax.axis_size("segment") - 1
        pairs = [(2 * (last - source) + at, 2 * last + 1 - at) for at in range(2)] + list(pairs)
        return lax.ppermute(array, ("segment", "band"), pairs)

    low = to_last(low, 4)
    high = to_last(high, 0, SWAP)

    slopes = ((rows - 1, wcol, C), F32)
    y1_far, slope1, slope2, edges2 = call(
        early, [some(rows - 1), slopes, slopes, some(2)],
        vmem(5), vmem(4), [map_rows(rows + 1)] * 3,
    )(one, two, first_input, weight_old, weight_now, two)
    edges2 = swapped(edges2)

    dx_near, y1, rest2, dz3_edge, maps, dz3 = call(
        backward_one,
        [
            some(rows + 1), some(rows + 1), some(rows - 2), ((2, wcol, 3 * C), BF16), some(rows + 4),
            ((rows + 3, wcol, 3 * C), BF16),
        ],
        vmem(9), vmem(6), [map_rows(4)],
    )(one, two, first_input, first_grad, edges, weight_old, weight_now, slope1, y1_far, two)
    returned_near = passed_along(dx_near, "segment", -1)
    x2 = passed_along(y1, "segment", 1)
    rest2 = swapped(rest2)
    (own_kgrad,) = call(own_kernel_grad, [(full, F32)], vmem(2), vmem(1), [])(maps, dz3, dx_near)

    dx_far, maps, dz3, next_grad_other = call(
        backward_one_rest,
        [some(rows - 1), some(rows + 2), ((rows + 1, wcol, 3 * C), BF16), some(rows)],
        vmem(7), vmem(4), [],
    )(one, edges, rest, dz3_edge, weight_old, low, high, own_kgrad)
    returned_far = passed_along(dx_far, "segment", -1)

    m_one, w_one = call(
        update_one, [(full, F32), ((1,) + full, BF16)], vmem(5), vmem(2), [],
    )(maps, dz3, own_kgrad, momentum, weight_now, dx_far)

    dx, own_kgrad, dz3_edge = call(
        backward_two,
        [some(rows), (full, F32), ((1, wcol, 3 * C), BF16)],
        vmem(7), vmem(3),
        [map_rows(rows + 3), map_rows(rows + 1), dz_rows(rows + 2)],
    )(
        two, edges2, returned_near, next_grad, next_grad_other,
        weight_now, slope2, m_one,
    )

    (act,) = call(forward_two, [some(rows)], vmem(4), vmem(1), [map_rows(rows + 2)])(
        next_kept, high, x2, w_one, dz3_edge
    )

    act, dx, m_two, w_two, w_one_out = call(
        finish,
        [((1, rows, wcol, C), BF16)] * 2 + [((1,) + full, F32)] + [((1,) + full, BF16)] * 2,
        vmem(12), hbm(5),
        [
            map_rows(rows + 2), map_rows(rows - 1), dz_rows(rows),
            pltpu.VMEM(full, F32), pltpu.VMEM(full, BF16), pltpu.SemaphoreType.DMA((9,)),
        ],
    )(
        two, edges2, rest2, dz3_edge, returned_far, next_grad_other,
        weight_now, own_kgrad, m_one, w_one, dx, act, act,
    )
    return act, dx, w_two, w_one_out, m_two


def fits_two_bands(mesh):
    return mesh.shape["band"] == 2 and mesh.shape["segment"] >= 8


def solution(mesh):
    placed = (
        P("segment", "band", None, None),
        P("segment", None, "band", None, None),
        P("segment", "band", None, None),
        P("segment", None, None, None, None),
        P("segment", None, None, None, None),
        P("segment", None, None, None, None),
        P(None, "segment"),
        P("band", None, None),
        P("band", None, None),
    )
    return jax.shard_map(
        two_band_body if fits_two_bands(mesh) else body,
        mesh=mesh,
        in_specs=placed,
        out_specs=(
            P("segment", "band", None, None),
            P("segment", "band", None, None),
            P("segment", None, None, None, None),
            P("segment", None, None, None, None),
            P("segment", None, None, None, None),
        ),
        check_vma=False,
    )
```

```python
import functools
import math

import jax
import jax.numpy as jnp
from jax import lax
from jax.experimental import pallas as pl
from jax.experimental.pallas import tpu as pltpu
from jax.sharding import PartitionSpec as P

C = 256


def padded_2(block, sides, width):
    for axis, dim in sides:
        count = lax.axis_size(axis)
        forward = [(i, i + 1) for i in range(count - 1)]
        backward = [(target, source) for source, target in forward]
        low = lax.ppermute(
            lax.slice_in_dim(block, block.shape[dim] - width, None, axis=dim), axis, forward
        )
        high = lax.ppermute(lax.slice_in_dim(block, 0, width, axis=dim), axis, backward)
        block = jnp.concatenate([low, block, high], axis=dim)
    return block


def passed_along(array, axis, by):
    length = lax.axis_size(axis)
    pairs = [(i, i + by) for i in range(length) if 0 <= i + by < length]
    return lax.ppermute(array, axis, pairs)


def row_patches(extended, rows):
    wcol = extended.shape[1]
    padded = jnp.pad(extended, ((0, 0), (1, 1), (0, 0)))
    taps = [padded[ky : ky + rows, kx : kx + wcol, :] for ky in range(3) for kx in range(3)]
    return jnp.concatenate(taps, axis=2).reshape(rows * wcol, -1)


def silu_slope(value):
    sig = jax.nn.sigmoid(value)
    return sig * (1.0 + value * (1.0 - sig))


def forward_part(x_in, flat_now, factor):
    rows, wcol = (x_in.shape[0], x_in.shape[1])
    ext = padded_2(x_in, (("band", 0),), 1)
    pre = jnp.dot(row_patches(ext, rows), flat_now, preferred_element_type=jnp.float32) * factor
    return jax.nn.silu(pre).astype(jnp.bfloat16).reshape(rows, wcol, C)


def backward_part(chosen, grad, w_old, factor):
    rows, wcol = (chosen.shape[0], chosen.shape[1])
    flat_old = w_old.reshape(9 * C, C)
    flip_old = w_old[::-1, ::-1].transpose(0, 1, 3, 2).reshape(9 * C, C)
    ext = padded_2(chosen, (("band", 0),), 1)
    patches = row_patches(ext, rows)
    back = jnp.dot(patches, flat_old, preferred_element_type=jnp.float32) * factor
    slope_grad = (grad.reshape(-1, C) * silu_slope(back)).astype(jnp.bfloat16)
    slope_ext = padded_2(slope_grad.reshape(rows, wcol, C), (("band", 0),), 1)
    kgrad = (
        lax.dot_general(
            patches, slope_grad, (((0,), (0,)), ((), ())), preferred_element_type=jnp.float32
        )
        * factor
    )
    in_grad = (
        jnp.dot(row_patches(slope_ext, rows), flip_old, preferred_element_type=jnp.float32) * factor
    )
    return (in_grad.astype(jnp.bfloat16).reshape(rows, wcol, C), kgrad)


def update_part(kgrad, w_now, moment):
    flat_now = w_now.reshape(9 * C, C).astype(jnp.float32)
    total = lax.psum(kgrad.astype(jnp.bfloat16), "band").astype(jnp.float32)
    new_moment = 0.9 * moment + total
    new_flat = (flat_now - 0.05 * new_moment).astype(jnp.bfloat16)
    return (new_flat.reshape(3, 3, C, C), new_moment)


def body(
    first_input,
    stashed,
    first_grad,
    weight_now,
    weight_old,
    momentum,
    slot_plan,
    next_input,
    next_grad,
):
    factor = 1.0 / math.sqrt(9 * C)
    segment_pos = lax.axis_index("segment")
    last_pos = lax.axis_size("segment") - 1
    x_in = first_input[0]
    stash = stashed[0]
    grad = first_grad[0]
    w_now = weight_now[0]
    w_old = weight_old[0]
    moment = momentum[0].reshape(9 * C, C)
    slots = slot_plan[:, 0]
    for tick in range(2):
        if tick == 1:
            arrived = passed_along(out_acts, "segment", 1)
            x_in = jnp.where(segment_pos == 0, next_input, arrived)
            returned = passed_along(in_grad, "segment", -1)
            grad = jnp.where(segment_pos == last_pos, next_grad, returned)
        out_acts = forward_part(x_in, w_now.reshape(9 * C, C), factor)
        chosen = lax.dynamic_index_in_dim(stash, slots[tick], 0, keepdims=False)
        in_grad, kgrad = backward_part(chosen, grad, w_old, factor)
        stash = lax.dynamic_update_index_in_dim(stash, x_in, slots[tick], 0)
        new_weight, moment = update_part(kgrad, w_now, moment)
        w_old = w_now
        w_now = new_weight
    return (out_acts[None], in_grad[None], w_now[None], w_old[None], moment.reshape(1, 3, 3, C, C))


SWAP = [(0, 1), (1, 0)]
BF16 = jnp.bfloat16
F32 = jnp.float32
NT = (((1,), (1,)), ((), ()))
TN = (((0,), (0,)), ((), ()))
MIB = 2**20


def vmem(count):
    return [pl.BlockSpec(memory_space=pltpu.VMEM)] * count


def anywhere(count):
    return [pl.BlockSpec(memory_space=pl.ANY)] * count


def hbm(count):
    return [pl.BlockSpec(memory_space=pltpu.HBM)] * count


SMEM = pl.BlockSpec(memory_space=pltpu.SMEM)


def call(kernel, outs, in_specs, out_specs, scratch, limit=24):
    count = len(in_specs)

    def ordered(*refs):
        kernel(lax.axis_index("band"), *refs[:count], *refs[count + 1 :])

    return pl.pallas_call(
        ordered,
        name=kernel.__name__,
        out_shape=[jax.ShapeDtypeStruct(shape, kind) for shape, kind in outs],
        in_specs=in_specs + anywhere(1),
        out_specs=out_specs,
        scratch_shapes=scratch,
        compiler_params=pltpu.CompilerParams(vmem_limit_bytes=limit * MIB),
        cost_estimate=pl.CostEstimate(flops=10**10, bytes_accessed=10**8, transcendentals=0),
    )


def conv_rows(rows_of, start, count, taps):
    lhs = [rows_of[pl.ds(start + ky, count)] for ky in range(3)]
    wcol = lhs[0].shape[1]
    lhs = jnp.concatenate([part.reshape(count * wcol, C) for part in lhs], axis=1)
    left, mid, right = (
        part.reshape(count, wcol, C) for part in (taps(lhs, 0), taps(lhs, 1), taps(lhs, 2))
    )
    col = lax.broadcasted_iota(jnp.int32, mid.shape, 1)
    left = jnp.where(col == 0, 0.0, pltpu.roll(left, 1, 1))
    right = jnp.where(col == wcol - 1, 0.0, pltpu.roll(right, wcol - 1, 1))
    return (left + mid + right) * (1.0 / math.sqrt(9 * C))


def on_either_side(me, part):
    for side in range(2):
        pl.when(me == side)(functools.partial(part, side))


def taps_of(kernel_ref):
    def taps(lhs, kx):
        rhs = jnp.concatenate([kernel_ref[0, ky, kx] for ky in range(3)], axis=0)
        return jnp.dot(lhs, rhs, preferred_element_type=F32)

    return taps


def flipped_taps_of(kernel_ref):
    def taps(lhs, kx):
        rhs = jnp.concatenate([kernel_ref[0, 2 - ky, 2 - kx] for ky in range(3)], axis=1)
        return lax.dot_general(lhs, rhs, NT, preferred_element_type=F32)

    return taps


def chunks(count):
    return [(at, min(2, count - at)) for at in range(0, count, 2)]


def silu_rows(maps, kernel_ref, count, out_ref, base=0):
    for at, size in chunks(count):
        pre = conv_rows(maps, base + at, size, taps_of(kernel_ref))
        out_ref[pl.ds(base + at, size)] = (pre / (1.0 + jnp.exp(-pre))).astype(BF16)


def slope_rows(maps, start, kernel_ref, count, store):
    for at, size in chunks(count):
        back = conv_rows(maps, start + at, size, taps_of(kernel_ref))
        sig = 1.0 / (1.0 + jnp.exp(-back))
        store(at, sig * (1.0 + back * (1.0 - sig)))


def put_dz(dz3, to, dz):
    wcol = dz.shape[1]
    col = lax.broadcasted_iota(jnp.int32, dz.shape, 1)
    row = pl.ds(to, dz.shape[0])
    dz3[row, :, 0:C] = jnp.where(col == 0, 0.0, pltpu.roll(dz, 1, 1)).astype(BF16)
    dz3[row, :, C : 2 * C] = dz.astype(BF16)
    dz3[row, :, 2 * C :] = jnp.where(
        col == wcol - 1, 0.0, pltpu.roll(dz, wcol - 1, 1)
    ).astype(BF16)


def dz_from(maps, start, kernel_ref, grads, grads_at, count, dz3, to):
    def job(at, size):
        def run():
            def store(_, slope):
                grad = grads[pl.ds(grads_at + at, size)].astype(F32)
                put_dz(dz3, to + at, grad * slope)

            slope_rows(maps, start + at, kernel_ref, size, store)

        return (to + at, size, run)

    return [job(at, size) for at, size in chunks(count)]


def dz_from_slopes(slopes, grads, grads_at, count, dz3, to):
    def job(at, size):
        def run():
            grad = grads[pl.ds(grads_at + at, size)].astype(F32)
            put_dz(dz3, to + at, grad * slopes[pl.ds(at, size)])

        return (to + at, size, run)

    return [job(at, size) for at, size in chunks(count)]


def dz_and_in_grad(jobs, there, dz3, kernel_ref, count, out_ref):
    there = set(there)
    waiting = chunks(count)
    for first, rows, run in jobs:
        run()
        there.update(range(first, first + rows))
        for at, size in list(waiting):
            if there.issuperset(range(at, at + size + 2)):
                dx = conv_rows(Middle(dz3), at, size, flipped_taps_of(kernel_ref))
                out_ref[pl.ds(at, size)] = dx.astype(BF16)
                waiting.remove((at, size))
    assert not waiting


class Middle:
    def __init__(self, dz3):
        self.dz3 = dz3

    def __getitem__(self, rows):
        return self.dz3[rows, :, C : 2 * C]


def kernel_grad(maps, start, dz3, dz_start, rows, ky):
    wcol = maps.shape[1]
    lhs = maps[pl.ds(start + ky, rows)].reshape(rows * wcol, C)
    rhs = dz3[pl.ds(dz_start, rows)].reshape(rows * wcol, 3 * C)
    grad = lax.dot_general(lhs, rhs, TN, preferred_element_type=F32) * (1.0 / math.sqrt(9 * C))
    return [grad[:, (2 - kx) * C : (3 - kx) * C] for kx in range(3)]


def zero_row(ref, at):
    ref[pl.ds(at, 1)] = jnp.zeros((1,) + ref.shape[1:], ref.dtype)


def put(ref, at, value):
    ref[pl.ds(at, value.shape[0])] = value


def put_second_map(ref, at, slots, x_in, stash):
    same = slots[0] == slots[1]

    @pl.when(same)
    def _():
        put(ref, at, x_in[0])

    @pl.when(jnp.logical_not(same))
    def _():
        put(ref, at, stash[0, slots[1]])


def edge(rows, count, me):
    return pl.ds((1 - me) * (rows - count), count)


def inner(rows, count, me):
    return pl.ds(me * (rows - count), count)


def start_copies(copies, sems, first):
    started = [
        pltpu.make_async_copy(a, b, sems.at[first + i]) for i, (a, b) in enumerate(copies)
    ]
    for copy in started:
        copy.start()
    return started


def pack(me, slots, x_in, stash, grad, edges, mark, sems):
    rows = stash.shape[2]
    mark[...] = jnp.zeros_like(mark)
    copies = start_copies(
        [
            (stash.at[0, slots[0], edge(rows, 3, me)], edges.at[pl.ds(0, 3)]),
            (grad.at[0, edge(rows, 2, me)], edges.at[pl.ds(3, 2)]),
            (x_in.at[0, edge(rows, 2, me)], edges.at[pl.ds(5, 2)]),
        ],
        sems, 0,
    )
    for copy in copies:
        copy.wait()


def pack_rest(
    me, slots, x_in, stash, grad, next_in, next_g, rest, one, two, next_kept, low, high
):
    rows = x_in.shape[1]
    one[...] = stash[0, slots[0]]
    put_second_map(two, 0, slots, x_in, stash)
    rest[0 : rows - 3] = one[inner(rows, rows - 3, me)]
    rest[rows - 3 :] = grad[0, inner(rows, rows - 2, me)]
    next_kept[...] = next_in[...]
    first = lax.axis_index("segment") == 0
    low[...] = next_g[0 : rows - 2]

    @pl.when(first)
    def _():
        high[...] = next_in[edge(rows, 2, me)]

    @pl.when(jnp.logical_not(first))
    def _():
        high[...] = next_g[rows - 2 :]


def early(
    me, one, two, x_in, w_old, w_now, y1, slope1, slope2, edges2, maps_x, maps_one, maps_two,
):
    rows = x_in.shape[1]
    edges2[...] = two[edge(rows, 2, me)]
    for maps, source in ((maps_x, x_in[0]), (maps_one, one[...]), (maps_two, two[...])):
        zero_row(maps, rows * me)
        put(maps, 1 - me, source)

    def keep(slopes, base):
        def store(at, slope):
            slopes[pl.ds(base + at, slope.shape[0])] = slope

        return store

    def looped(step):
        pairs = (rows - 1) // 2
        lax.fori_loop(0, pairs, lambda at, _: step(2 * at, 2), None)
        if (rows - 1) % 2:
            step(2 * pairs, 1)

    looped(lambda at, size: slope_rows(maps_two, at, w_now, size, keep(slope2, at)))
    looped(lambda at, size: slope_rows(maps_one, at, w_old, size, keep(slope1, at)))
    looped(lambda at, size: silu_rows(maps_x, w_now, size, y1, at))


def forward_two(me, next_in, beside, arrived, w_one, act, maps):
    first = lax.axis_index("segment") == 0
    rows = next_in.shape[0]
    zero_row(maps, (rows + 1) * me)

    @pl.when(first)
    def _():
        put(maps, 1, next_in[...])
        put(maps, (rows + 1) * (1 - me), beside[pl.ds(me, 1)])

    @pl.when(jnp.logical_not(first))
    def _():
        put(maps, 1 - me, arrived[...])

    silu_rows(maps, w_one, rows, act)


def backward_one(
    me, one, two, x_in, grad, edges, w_old, w_now, slope1, y1_far,
    dx, y1, rest2, dz3_edge, maps, dz3, border,
):
    rows = one.shape[0]
    rest2[...] = two[inner(rows, rows - 2, me)]
    put(border, 2 * me, x_in[0, edge(rows, 2, me)])
    put(border, 2 * (1 - me), edges[5:7])
    silu_rows(border, w_now, 2, y1.at[pl.ds((rows - 1) * (1 - me), 2)])
    put(y1, 2 * me, y1_far[...])
    zero_row(maps, (rows + 3) * me)
    put(maps, 1 + 2 * me, one[...])
    put(maps, (rows + 1) * (1 - me), edges[0:3])
    zero_row(dz3, (rows + 2) * me)

    def part(me):
        own = 1 + me
        near = own + (rows - 1) * (1 - me)
        other = own + rows * (1 - me) - 2 * me
        jobs = dz_from(maps, near - 1 + me, w_old, grad.at[0], (rows - 1) * (1 - me), 1, dz3, near)
        jobs += dz_from(maps, other - 1 + me, w_old, edges, 3, 2, dz3, other)
        jobs += dz_from_slopes(slope1, grad.at[0], me, rows - 1, dz3, own + me)
        dz_and_in_grad(jobs, [(rows + 2) * me], dz3, w_old, rows + 1, dx)

    on_either_side(me, part)
    dz3_edge[...] = dz3[pl.ds((rows + 1) * (1 - me), 2)]


def keep_kernel_grad(maps, start, dz3, dz_start, rows, out, unroll):
    def step(ky, _):
        taps = kernel_grad(maps, start, dz3, dz_start, rows, ky)
        for kx in range(3):
            out[ky, kx] = taps[kx]

    lax.fori_loop(0, 3, step, None, unroll=unroll)


def own_kernel_grad(me, maps, dz3, own_kgrad):
    rows = maps.shape[0] - 4
    keep_kernel_grad(maps, 2 * me, dz3, 1 + me, rows, own_kgrad, 1)


def backward_one_rest(
    me, one, edges, rest, dz3_edge, w_old, low, high, dx, maps, dz3, next_g_other
):
    rows = one.shape[0]
    zero_row(maps, (rows + 1) * (1 - me))
    put(next_g_other, 0, low[...])
    put(next_g_other, rows - 2, high[...])
    put(maps, (rows + 1) * me, one[edge(rows, 1, me)])
    put(maps, 1 + (rows - 3) * me, edges[0:3])
    put(maps, 4 - 3 * me, rest[0 : rows - 3])
    zero_row(dz3, rows * (1 - me))
    put(dz3, (rows - 1) * me, dz3_edge[...])

    def part(me):
        jobs = dz_from(maps, 2 * (1 - me), w_old, rest, rows - 3, rows - 2, dz3, 2 - me)
        there = [rows * (1 - me), (rows - 1) * me, (rows - 1) * me + 1]
        dz_and_in_grad(jobs, there, dz3, w_old, rows - 1, dx)

    on_either_side(me, part)


def update_one(me, maps, dz3, own_kgrad, moment, w_now, m_one, w_one):
    rows = maps.shape[0] - 2

    def step(ky, _):
        taps = kernel_grad(maps, 0, dz3, me, rows, ky)
        for kx in range(3):
            fresh = 0.9 * moment[0, ky, kx] + (own_kgrad[ky, kx] + taps[kx])
            m_one[ky, kx] = fresh
            w_one[0, ky, kx] = (w_now[0, ky, kx].astype(F32) - 0.05 * fresh).astype(BF16)

    lax.fori_loop(0, 3, step, None)


def backward_two(
    me, two, edges2, returned, next_g, next_g_other, w_now, slope2,
    dx, own_kgrad, dz3_edge, maps, grads, dz3,
):
    last = lax.axis_index("segment") == lax.axis_size("segment") - 1
    rows = two.shape[0]
    zero_row(maps, (rows + 2) * me)
    put(maps, 1 + me, two[...])
    put(maps, (rows + 1) * (1 - me), edges2[...])

    @pl.when(last)
    def _():
        put(grads, me, next_g[...])
        put(grads, rows * (1 - me), next_g_other[pl.ds((rows - 1) * me, 1)])

    @pl.when(jnp.logical_not(last))
    def _():
        put(grads, 0, returned[...])

    zero_row(dz3, (rows + 1) * me)

    def part(me):
        near = (rows - 1) * (1 - me)
        jobs = dz_from(maps, near, w_now, grads, near, 2, dz3, near + 1 - me)
        jobs += dz_from_slopes(slope2, grads, 2 * me, rows - 1, dz3, 1 + me)
        dz_and_in_grad(jobs, [(rows + 1) * me], dz3, w_now, rows, dx)

    on_either_side(me, part)
    dz3_edge[...] = dz3[pl.ds((rows + 1) * (1 - me), 1)]
    keep_kernel_grad(maps, me, dz3, 1, rows, own_kgrad, 3)


def finish(
    me, two, edges2, rest2, dz3_edge, returned, next_g_other, w_now,
    own_kgrad, m_one, w_one, dx, act,
    act_out, dx_out, m_out, w_out, w_one_out, maps, grads, dz3, m_two, w_two, sems,
):
    last = lax.axis_index("segment") == lax.axis_size("segment") - 1
    rows = two.shape[0]
    copies = start_copies(
        [(act, act_out.at[0]), (w_one, w_one_out), (dx, dx_out.at[0])], sems, 6
    )
    zero_row(maps, (rows + 1) * (1 - me))
    put(maps, (rows + 1) * me, two[edge(rows, 1, me)])
    put(maps, 1 + (rows - 2) * me, edges2[...])
    put(maps, 3 - 2 * me, rest2[...])

    @pl.when(last)
    def _():
        put(grads, 0, next_g_other[pl.ds(1 - me, rows - 1)])

    @pl.when(jnp.logical_not(last))
    def _():
        put(grads, 0, returned[...])

    put(dz3, (rows - 1) * me, dz3_edge[...])
    for _, _, run in dz_from(maps, 1 - me, w_now, grads, 0, rows - 1, dz3, 1 - me):
        run()

    def outputs(ky):
        return [(m_two.at[ky], m_out.at[0, ky]), (w_two.at[ky], w_out.at[0, ky])]

    def step(ky, _):
        taps = kernel_grad(maps, 0, dz3, 0, rows, ky)
        for kx in range(3):
            fresh = 0.9 * m_one[ky, kx] + (own_kgrad[ky, kx] + taps[kx])
            m_two[ky, kx] = fresh
            w_two[ky, kx] = (w_one[0, ky, kx].astype(F32) - 0.05 * fresh).astype(BF16)
        copies.extend(start_copies(outputs(ky), sems, 2 * ky))

    for ky in range(3):
        step(ky, None)
    for copy in copies:
        copy.wait()


def two_band_body(
    first_input, stashed, first_grad, weight_now, weight_old, momentum, slot_plan,
    next_input, next_grad,
):
    rows, wcol = first_input.shape[1:3]
    unit = rows * wcol * 9 * C * C
    full = (3, 3, C, C)

    def some(count):
        return ((count, wcol, C), BF16)

    def map_rows(count):
        return pltpu.VMEM((count, wcol, C), BF16)

    def dz_rows(count):
        return pltpu.VMEM((count, wcol, 3 * C), BF16)

    def swapped(array):
        return lax.ppermute(array, "band", SWAP)

    slots = slot_plan.reshape(2)
    edges, mark = call(
        pack, [some(7), ((8, 128), F32)], [SMEM] + hbm(3), vmem(2),
        [pltpu.SemaphoreType.DMA((3,))], 56,
    )(slots, first_input, stashed, first_grad, slots)
    edges = swapped(edges)

    rest, one, two, next_kept, low, high = call(
        pack_rest, [some(2 * rows - 5)] + [some(rows)] * 3 + [some(rows - 2), some(2)],
        [SMEM] + vmem(5), vmem(6), [],
    )(slots, first_input, stashed, first_grad, next_input, next_grad, mark)
    rest = swapped(rest)

    def to_last(array, source, pairs=()):
        last = lax.axis_size("segment") - 1
        pairs = [(2 * (last - source) + at, 2 * last + 1 - at) for at in range(2)] + list(pairs)
        return lax.ppermute(array, ("segment", "band"), pairs)

    low = to_last(low, 2)
    high = to_last(high, 0, SWAP)

    slopes = ((rows - 1, wcol, C), F32)
    y1_far, slope1, slope2, edges2 = call(
        early, [some(rows - 1), slopes, slopes, some(2)],
        vmem(5), vmem(4), [map_rows(rows + 1)] * 3,
    )(one, two, first_input, weight_old, weight_now, two)
    edges2 = swapped(edges2)

    dx_near, y1, rest2, dz3_edge, maps, dz3 = call(
        backward_one,
        [
            some(rows + 1), some(rows + 1), some(rows - 2), ((2, wcol, 3 * C), BF16), some(rows + 4),
            ((rows + 3, wcol, 3 * C), BF16),
        ],
        vmem(9), vmem(6), [map_rows(4)],
    )(one, two, first_input, first_grad, edges, weight_old, weight_now, slope1, y1_far, two)
    returned_near = passed_along(dx_near, "segment", -1)
    x2 = passed_along(y1, "segment", 1)
    rest2 = swapped(rest2)
    (own_kgrad,) = call(own_kernel_grad, [(full, F32)], vmem(2), vmem(1), [])(maps, dz3, dx_near)

    dx_far, maps, dz3, next_grad_other = call(
        backward_one_rest,
        [some(rows - 1), some(rows + 2), ((rows + 1, wcol, 3 * C), BF16), some(rows)],
        vmem(7), vmem(4), [],
    )(one, edges, rest, dz3_edge, weight_old, low, high, own_kgrad)
    returned_far = passed_along(dx_far, "segment", -1)

    m_one, w_one = call(
        update_one, [(full, F32), ((1,) + full, BF16)], vmem(5), vmem(2), [],
    )(maps, dz3, own_kgrad, momentum, weight_now, dx_far)

    dx, own_kgrad, dz3_edge = call(
        backward_two,
        [some(rows), (full, F32), ((1, wcol, 3 * C), BF16)],
        vmem(7), vmem(3),
        [map_rows(rows + 3), map_rows(rows + 1), dz_rows(rows + 2)],
    )(
        two, edges2, returned_near, next_grad, next_grad_other,
        weight_now, slope2, m_one,
    )

    (act,) = call(forward_two, [some(rows)], vmem(4), vmem(1), [map_rows(rows + 2)])(
        next_kept, high, x2, w_one, dz3_edge
    )

    act, dx, m_two, w_two, w_one_out = call(
        finish,
        [((1, rows, wcol, C), BF16)] * 2 + [((1,) + full, F32)] + [((1,) + full, BF16)] * 2,
        vmem(12), hbm(5),
        [
            map_rows(rows + 2), map_rows(rows - 1), dz_rows(rows),
            pltpu.VMEM(full, F32), pltpu.VMEM(full, BF16), pltpu.SemaphoreType.DMA((9,)),
        ],
    )(
        two, edges2, rest2, dz3_edge, returned_far, next_grad_other,
        weight_now, own_kgrad, m_one, w_one, dx, act, act,
    )
    return act, dx, w_two, w_one_out, m_two


def fits_two_bands(mesh):
    return mesh.shape["band"] == 2 and mesh.shape["segment"] >= 8


def solution(mesh):
    placed = (
        P("segment", "band", None, None),
        P("segment", None, "band", None, None),
        P("segment", "band", None, None),
        P("segment", None, None, None, None),
        P("segment", None, None, None, None),
        P("segment", None, None, None, None),
        P(None, "segment"),
        P("band", None, None),
        P("band", None, None),
    )
    return jax.shard_map(
        two_band_body if fits_two_bands(mesh) else body,
        mesh=mesh,
        in_specs=placed,
        out_specs=(
            P("segment", "band", None, None),
            P("segment", "band", None, None),
            P("segment", None, None, None, None),
            P("segment", None, None, None, None),
            P("segment", None, None, None, None),
        ),
        check_vma=False,
    )
```
